32 devices in a mesh: ctx: 4 (over y, x), chan: 8 (over z, core).
Axes of the slice: x: 2, y: 2, z: 4, core: 2. Of those that a mesh axis runs over, the one named last changes fastest.
Arguments:
- inputs: bfloat16 [2048, 4096], P('ctx', 'chan'), may hold values from -6 to 6
- w_in: bfloat16 [4096, 3, 4096], P(None, None, 'chan'), may hold values from -0.09375 to 0.09375
- conv_taps: bfloat16 [3, 3, 4096], P(None, None, 'chan'), may hold values from -3.59375 to 3.59375
- skip_gain: float32 [4096], P('chan'), may hold values from 0.5 to 1.5
- filter_taps: bfloat16 [2048, 4096], P('ctx', 'chan'), may hold values from -0.125 to 0.125
- w_out: bfloat16 [4096, 4096], P('chan'), may hold values from -0.125 to 0.125
Outputs:
- result: bfloat16 [2048, 4096], P('ctx', 'chan')
The draws below stay inside these ranges and needn't reach their ends.
All inputs are finite; a program needn't handle non-finite values.
Results may differ from the reference program's by a relative error of at most 0.024.
Values may be sent and summed in bfloat16 or wider, within the bound.
No kernel may reach another device: no remote copies, remote signals or barrier semaphores. Data moves between devices by JAX's collectives and lax.ppermute only.
A program may use at most 128 MiB of HBM per device.

```python
import math
import jax
import jax.numpy as jnp

D = 4096
KERNEL = 3
SPAN = 512
LEN = 2048
N_CTX = 4


def spiked(result, key, source, target, shards_of, factor):
    owner, partner = [(jnp.arange(result.shape[axis_at]) // (result.shape[axis_at] // shards_of)).reshape([-1 if axis == axis_at else 1 for axis in range(result.ndim)]) for axis_at in (source, target)]
    chosen = jax.random.permutation(key, shards_of)[partner]
    strong = (owner == chosen) | (owner == (partner + shards_of // 2) % shards_of)
    return jnp.where(strong, factor * result, result)


def block_levels(key, extent, pieces, smallest, high):
    def one(dim, parts):
        draws = jax.random.uniform(jax.random.fold_in(jax.random.fold_in(key, 6), dim), (parts,), jnp.float32, smallest / len(pieces), high / len(pieces))
        return jnp.repeat(jnp.exp(draws), extent[dim] // parts).reshape((-1,) + (1,) * (len(extent) - dim - 1))

    gain = one(*pieces[0])
    for cut in pieces[1:]:
        gain = gain * one(*cut)
    return gain


def noise(rng, extent, scale, most, split=(), kind=jnp.bfloat16):
    gain = block_levels(rng, extent, split, -0.22, 0.18) if split else 1.0
    entries = jax.random.normal(rng, extent, jnp.float32) * scale * gain
    return jnp.minimum(jnp.maximum(entries, -most), most).astype(kind)


def bell_draw_with(stream_key, shape, deviation, bound, shards, heavy, kind=jnp.bfloat16):
    entries = deviation * jax.random.normal(stream_key, shape, jnp.float32)
    if shards:
        entries = entries * block_levels(stream_key, shape, shards, -0.22, 0.18)
    return jnp.clip(spiked(entries, jax.random.fold_in(stream_key, 3), *heavy), -bound, bound).astype(kind)


def setup_inputs(seed: int = 0) -> dict:
    key_of = jax.random.split(jax.random.key(seed), 7)
    inputs = noise(key_of[0], (LEN, D), 1.0, 6.0, ((0, 4), (1, 8)))
    w_in = noise(key_of[1], (D, 3, D), D ** -0.5, 0.09375, ((2, 8),))
    conv_taps = noise(key_of[2], (KERNEL, 3, D), 0.6, 3.59375, ((2, 8),))
    skip_gain = jnp.clip(0.5 + 1.0 * jax.random.uniform(key_of[3], (D,), jnp.float32) ** block_levels(key_of[3], (D,), ((0, 8),), -0.2, 0.2), 0.5, 1.5)
    filter_taps = noise(key_of[4], (LEN, D), LEN ** -0.5, 0.125, ((0, 4), (1, 8)))
    w_out = bell_draw_with(key_of[5], (D, D), D ** -0.5, 0.125, ((0, 8),), (0, 1, 8, 2.0))
    return dict(inputs=inputs, w_in=w_in, conv_taps=conv_taps, skip_gain=skip_gain, filter_taps=filter_taps, w_out=w_out)


def angles(row_count, col_count, double_len):
    row_ids = jnp.arange(row_count, dtype=jnp.int32)[:, None]
    col_ids = jnp.arange(col_count, dtype=jnp.int32)[None, :]
    return (2.0 * math.pi / double_len) * ((row_ids * col_ids) % double_len).astype(jnp.float32)


def tables(span_len):
    double_len = 2 * span_len
    first = angles(double_len, span_len, double_len)
    forward_in = jnp.concatenate([jnp.cos(first), -jnp.sin(first)], 0).astype(jnp.bfloat16)
    second = angles(double_len, double_len, double_len)
    forward_taps = jnp.concatenate([jnp.cos(second), -jnp.sin(second)], 0).astype(jnp.bfloat16)
    third = angles(span_len, double_len, double_len)
    inverse = (jnp.concatenate([jnp.cos(third), -jnp.sin(third)], 1) / double_len).astype(jnp.bfloat16)
    return forward_in, forward_taps, inverse


def spectral_product(taps_spec, input_spec, double_len):
    real_g = taps_spec[:double_len].astype(jnp.float32)
    imag_g = taps_spec[double_len:].astype(jnp.float32)
    real_u = input_spec[:double_len].astype(jnp.float32)
    imag_u = input_spec[double_len:].astype(jnp.float32)
    return jnp.concatenate([real_g * real_u - imag_g * imag_u, real_g * imag_u + imag_g * real_u], 0)


def reference(inputs, w_in, conv_taps, skip_gain, filter_taps, w_out):
    span_len = SPAN
    double_len = 2 * span_len
    projected = jnp.dot(inputs, w_in.reshape(D, 3 * D), preferred_element_type=jnp.float32)
    projected = projected.astype(jnp.bfloat16).reshape(LEN, 3, D)
    padded = jnp.concatenate([jnp.zeros((KERNEL - 1, 3, D), jnp.bfloat16), projected], 0)
    filtered = jnp.zeros((LEN, 3, D), jnp.float32)
    for lag in range(KERNEL):
        start_row = KERNEL - 1 - lag
        filtered = filtered + conv_taps[lag].astype(jnp.float32) * padded[start_row:start_row + LEN].astype(jnp.float32)
    streams = filtered.astype(jnp.bfloat16)
    gate_out = streams[:, 0]
    gated_in = (streams[:, 1].astype(jnp.float32) * streams[:, 2].astype(jnp.float32)).astype(jnp.bfloat16)
    forward_in, forward_taps, inverse = tables(span_len)
    blocks = gated_in.reshape(N_CTX, span_len, D)
    spectra_in = jnp.einsum("fb,kbd->kfd", forward_in.astype(jnp.float32), blocks.astype(jnp.float32)).astype(jnp.bfloat16)
    lag_blocks = filter_taps.reshape(N_CTX, span_len, D)
    previous = jnp.concatenate([jnp.zeros((1, span_len, D), jnp.bfloat16), lag_blocks[:-1]], 0)
    padded_taps = jnp.concatenate([lag_blocks, jnp.zeros((N_CTX, 1, D), jnp.bfloat16), previous[:, 1:]], 1)
    spectra_taps = jnp.einsum("fm,kmd->kfd", forward_taps.astype(jnp.float32), padded_taps.astype(jnp.float32)).astype(jnp.bfloat16)
    outputs = []
    for target in range(N_CTX):
        mixture = jnp.zeros((2 * double_len, D), jnp.float32)
        for source in range(target + 1):
            mixture = mixture + spectral_product(spectra_taps[target - source], spectra_in[source], double_len)
        long_out = jnp.dot(inverse, mixture.astype(jnp.bfloat16), preferred_element_type=jnp.float32)
        long_out = long_out + skip_gain.astype(jnp.float32) * blocks[target].astype(jnp.float32)
        gate_rows = gate_out[target * span_len:(target + 1) * span_len].astype(jnp.float32)
        outputs.append((gate_rows * long_out).astype(jnp.bfloat16))
    gated_out = jnp.concatenate(outputs, 0)
    return jnp.dot(gated_out, w_out, preferred_element_type=jnp.float32).astype(jnp.bfloat16)
```

```python
import math

import jax
import jax.numpy as jnp
import ml_dtypes
import numpy as np
from jax import lax
from jax.sharding import PartitionSpec as P

KERNEL = 3
BF16 = jnp.bfloat16
F32 = jnp.float32


def half_tables(span):
    n = 2 * span
    f = np.arange(span)[:, None]
    m = np.arange(n)[None, :]
    ang = 2.0 * math.pi * ((f * m) % n) / n
    real = np.cos(ang)
    imag = -np.sin(ang)
    imag[0] = np.where(np.arange(n) % 2 == 0, 1.0, -1.0)
    forward = np.concatenate([real, imag], 0).astype(ml_dtypes.bfloat16)
    weight = np.full((n, 1), 2.0 / n)
    weight[0] = 1.0 / n
    weight[span] = 1.0 / n
    back = (np.concatenate([real, imag], 0) * weight)[:, :span].T
    return forward, np.ascontiguousarray(back).astype(ml_dtypes.bfloat16)


def shift(x, axis, distance):
    size = lax.axis_size(axis)
    return lax.ppermute(x, axis, [(i, (i + distance) % size) for i in range(size)])


def sibling(x):
    return lax.ppermute(x, "chan", [(i, i ^ 1) for i in range(lax.axis_size("chan"))])


def dot(a, b):
    return jnp.dot(a, b, preferred_element_type=F32)


def gather_chips(x):
    chips = lax.axis_size("chan") // 2
    half = x.shape[0] // 2
    top, low = x[:half], x[half:]
    found = []
    up = [top, low]
    down = [top, low]
    for d in range(1, chips // 2 + 1):
        if 2 * d < chips:
            up = [shift(v, "chan", 2) for v in up]
            down = [shift(v, "chan", -2) for v in down]
            found.append((d, up))
            found.append((-d, down))
        else:
            found.append((d, [shift(up[0], "chan", 2), shift(down[1], "chan", -2)]))
    return found


def exchange(pieces):
    groups = lax.axis_size("ctx")
    me = lax.axis_index("ctx")
    out = [(me, pieces(me))]
    for s in range(1, groups):
        out.append(((me - s) % groups, shift(pieces((me + s) % groups), "ctx", s)))
    return out


def in_order(found):
    groups = len(found)
    block = found[0][1]
    whole = jnp.zeros((groups,) + block.shape, block.dtype)
    for source, b in found:
        whole = lax.dynamic_update_index_in_dim(whole, b, source, 0)
    return whole


def body(inputs, w_in, conv_taps, skip_gain, filter_taps, w_out):
    span, width = inputs.shape
    n = 2 * span
    groups = lax.axis_size("ctx")
    me = lax.axis_index("ctx")
    chan = lax.axis_size("chan")
    chips = chan // 2
    place = lax.axis_index("chan")
    chip, core = place // 2, place % 2
    quarter = width // groups
    forward_np, back_np = half_tables(span)
    forward, back = jnp.asarray(forward_np), jnp.asarray(back_np)

    found = gather_chips(inputs)

    taps = jnp.stack(jnp.split(filter_taps, groups, axis=1))
    taps = in_order(
        exchange(lambda q: lax.dynamic_index_in_dim(taps, q, 0, keepdims=False))
    )
    taps = jnp.concatenate(list(taps), 1)
    row_ids = lax.broadcasted_iota(jnp.int32, (span, 1), 0)
    before = jnp.concatenate(
        [jnp.zeros((span, quarter), BF16), taps[:, : (groups - 1) * quarter]], 1
    )
    before = jnp.where(row_ids == 0, 0, before)
    spectra_taps = dot(forward, jnp.concatenate([taps, before], 0)).astype(BF16)

    w_split = w_out.reshape(width, chips, 2, -1)
    mine = lax.dynamic_index_in_dim(w_split, core, 2, keepdims=False)
    theirs = sibling(lax.dynamic_index_in_dim(w_split, 1 - core, 2, keepdims=False))

    w_flat = w_in.reshape(w_in.shape[0], 3 * width)

    def part(block, chip_id, core_id):
        rows = lax.dynamic_slice_in_dim(w_flat, (chip_id * 2 + core_id) * width, width, 0)
        return dot(block, rows)

    total = part(inputs, chip, core) + part(sibling(inputs), chip, 1 - core)
    for d, (top, low) in found:
        block = jnp.concatenate([top, low], 0)
        source = (chip - d) % chips
        total = total + part(block, source, core)
        total = total + part(sibling(block), source, 1 - core)
    projected = total.astype(BF16)

    rim = shift(projected[span - (KERNEL - 1) :], "ctx", 1)
    rim = jnp.where(me > 0, rim, 0)
    padded = jnp.concatenate([rim, projected], 0)
    filtered = jnp.zeros((span, 3 * width), F32)
    flat_taps = conv_taps.reshape(KERNEL, 3 * width).astype(F32)
    for lag in range(KERNEL):
        first = KERNEL - 1 - lag
        filtered = filtered + flat_taps[lag] * padded[first : first + span].astype(F32)
    streams = filtered.astype(BF16)
    gate_out = streams[:, :width]
    gated_in = (
        streams[:, width : 2 * width].astype(F32) * streams[:, 2 * width :].astype(F32)
    ).astype(BF16)

    split_in = jnp.stack(jnp.split(gated_in, groups, axis=1))
    signal = in_order(
        exchange(lambda q: lax.dynamic_index_in_dim(split_in, q, 0, keepdims=False))
    )
    signal = jnp.concatenate(list(signal), 1)
    spectra_in = dot(forward[:, :span], signal).astype(BF16)
    real_g = spectra_taps[:span].astype(F32)
    imag_g = spectra_taps[span:].astype(F32)
    real_u = spectra_in[:span].astype(F32)
    imag_u = spectra_in[span:].astype(F32)
    first_row = row_ids == 0
    mixed = []
    for i in range(groups):
        real = jnp.zeros((span, quarter), F32)
        imag = jnp.zeros((span, quarter), F32)
        for j in range(i + 1):
            g = slice((i - j) * quarter, (i - j + 1) * quarter)
            u = slice(j * quarter, (j + 1) * quarter)
            rr = real_g[:, g] * real_u[:, u]
            ii = imag_g[:, g] * imag_u[:, u]
            ri = real_g[:, g] * imag_u[:, u] + imag_g[:, g] * real_u[:, u]
            real = real + jnp.where(first_row, rr, rr - ii)
            imag = imag + jnp.where(first_row, ii, ri)
        mixed.append(jnp.concatenate([real, imag], 0).astype(BF16))
    mixture = jnp.concatenate(mixed, 1)
    long_share = dot(back, mixture).astype(BF16)
    long_share = jnp.stack(jnp.split(long_share, groups, axis=1))
    long_out = in_order(
        exchange(lambda q: lax.dynamic_index_in_dim(long_share, q, 0, keepdims=False))
    )
    long_out = jnp.concatenate(list(long_out), 1).astype(F32)
    long_out = long_out + skip_gain * gated_in.astype(F32)
    gated_out = (gate_out.astype(F32) * long_out).astype(BF16)

    other = sibling(gated_out)

    def share(chip_id, rows=slice(None)):
        a = lax.dynamic_index_in_dim(mine, chip_id, 1, keepdims=False)
        b = lax.dynamic_index_in_dim(theirs, chip_id, 1, keepdims=False)
        return dot(gated_out[rows], a) + dot(other[rows], b)

    half = span // 2
    top, low = slice(0, half), slice(half, span)
    up = [None, None]
    down = [None, None]

    def carry(old, new):
        return new if old is None else old.astype(F32) + new

    for d in range(chips // 2, 0, -1):
        if 2 * d < chips:
            ahead, behind = (chip + d) % chips, (chip - d) % chips
            up = [
                shift(carry(u, share(ahead, r)).astype(BF16), "chan", 2)
                for u, r in zip(up, (top, low))
            ]
            down = [
                shift(carry(u, share(behind, r)).astype(BF16), "chan", -2)
                for u, r in zip(down, (top, low))
            ]
        else:
            far = (chip + d) % chips
            up[0] = shift(share(far, top).astype(BF16), "chan", 2)
            down[1] = shift(share(far, low).astype(BF16), "chan", -2)
    result = []
    for k, r in enumerate((top, low)):
        total = share(chip, r)
        for extra in (up[k], down[k]):
            if extra is not None:
                total = total + extra.astype(F32)
        result.append(total.astype(BF16))
    return jnp.concatenate(result, 0)


def solution(mesh):
    return jax.shard_map(
        body,
        mesh=mesh,
        in_specs=(
            P("ctx", "chan"),
            P(None, None, "chan"),
            P(None, None, "chan"),
            P("chan"),
            P("ctx", "chan"),
            P("chan", None),
        ),
        out_specs=P("ctx", "chan"),
        check_vma=False,
    )
```

```python
import math

import jax
import jax.numpy as jnp
import ml_dtypes
import numpy as np
from jax import lax
from jax.experimental import pallas as pl
from jax.experimental.pallas import tpu as pltpu
from jax.sharding import PartitionSpec as P

KERNEL = 3
RIM = 8
BF16 = jnp.bfloat16
F32 = jnp.float32
MIB = 1 << 20


def half_tables(span):
    n = 2 * span
    f = np.arange(span)[:, None]
    m = np.arange(n)[None, :]
    ang = 2.0 * math.pi * ((f * m) % n) / n
    real = np.cos(ang)
    imag = -np.sin(ang)
    imag[0] = np.where(np.arange(n) % 2 == 0, 1.0, -1.0)
    forward = np.concatenate([real, imag], 0).astype(ml_dtypes.bfloat16)
    weight = np.full((n, 1), 2.0 / n)
    weight[0] = 1.0 / n
    weight[span] = 1.0 / n
    back = (np.concatenate([real, imag], 0) * weight)[:, :span].T
    return forward, np.ascontiguousarray(back).astype(ml_dtypes.bfloat16)


def shift(x, axis, distance):
    size = lax.axis_size(axis)
    return lax.ppermute(x, axis, [(i, (i + distance) % size) for i in range(size)])


def sibling(x):
    return lax.ppermute(x, "chan", [(i, i ^ 1) for i in range(lax.axis_size("chan"))])


def dot(a, b):
    return jnp.dot(a, b, preferred_element_type=F32)


def after(x, *others):
    return lax.optimization_barrier((x,) + others)[0]


def whole(shape):
    return pl.BlockSpec(shape, lambda *_: (0,) * len(shape))


def call(kernel, grid, prefetch, operands, in_specs, outs, out_specs, scratch, name, flops, moved):
    return pl.pallas_call(
        kernel,
        grid_spec=pltpu.PrefetchScalarGridSpec(
            num_scalar_prefetch=1,
            grid=grid,
            in_specs=in_specs,
            out_specs=out_specs,
            scratch_shapes=scratch,
        ),
        out_shape=outs,
        compiler_params=pltpu.CompilerParams(vmem_limit_bytes=32 * MIB),
        cost_estimate=pl.CostEstimate(flops=flops, bytes_accessed=moved, transcendentals=0),
        name=name,
    )(prefetch, *operands)


def project(pairs, chip_ids, core, w_in, conv_taps, groups, total=None, finish=False):
    count = len(pairs)
    rows, width = pairs[0][0].shape
    streams, _, out_width = w_in.shape
    kept = rows - RIM
    split = out_width // groups % 128 == 0
    share = out_width // groups
    blocks = [b for pair in pairs for b in pair]
    has_total = total is not None

    def kernel(ids, w_ref, *refs):
        x_refs, refs = refs[: 2 * count], refs[2 * count :]
        if has_total:
            total_ref, refs = refs[0], refs[1:]
        if finish:
            taps_ref, gate_ref, in_ref, acc = refs
        else:
            acc = refs[0]
        k, s = pl.program_id(0), pl.program_id(1)
        mine = pl.multiple_of(ids[count] * width, width)
        theirs = pl.multiple_of((1 - ids[count]) * width, width)
        for j in range(count):

            @pl.when(k == j)
            def _():
                part = dot(x_refs[2 * j][...], w_ref[0, pl.ds(mine, width)])
                part = part + dot(x_refs[2 * j + 1][...], w_ref[0, pl.ds(theirs, width)])
                if j > 0:
                    part = part + acc[s]
                elif has_total:
                    part = part + total_ref[s]
                acc[s] = part

        if finish:

            @pl.when((k == count - 1) & (s == streams - 1))
            def _():
                def filtered(t):
                    rounded = acc[t].astype(BF16).astype(F32)
                    result = jnp.zeros((kept, out_width), F32)
                    for lag in range(KERNEL):
                        row = lag * streams + t
                        result = result + taps_ref[row : row + 1, :] * rounded[RIM - lag : rows - lag]
                    return result.astype(BF16)

                gate_ref[...] = filtered(0)
                gated = (filtered(1).astype(F32) * filtered(2).astype(F32)).astype(BF16)
                if split:
                    for q in range(groups):
                        in_ref[q] = gated[:, q * share : (q + 1) * share]
                else:
                    in_ref[...] = gated

    in_specs = [pl.BlockSpec((1, 2 * width, out_width), lambda k, s, ids: (s, ids[k], 0))]
    in_specs += [whole(b.shape) for b in blocks]
    operands = [w_in] + blocks
    if has_total:
        in_specs.append(whole(total.shape))
        operands.append(total)
    acc_shape = (streams, rows, out_width)
    if finish:
        in_specs.append(whole(conv_taps.shape))
        operands.append(conv_taps)
        in_shape = (groups, kept, share) if split else (kept, out_width)
        outs = [
            jax.ShapeDtypeStruct((kept, out_width), BF16),
            jax.ShapeDtypeStruct(in_shape, BF16),
        ]
        scratch = [pltpu.VMEM(acc_shape, F32)]
    else:
        outs = [jax.ShapeDtypeStruct(acc_shape, F32)]
        scratch = []
    return call(
        kernel,
        (count, streams),
        jnp.stack(list(chip_ids) + [core]).astype(jnp.int32),
        operands,
        in_specs,
        outs,
        [whole(o.shape) for o in outs],
        scratch,
        "project",
        4 * count * rows * width * streams * out_width,
        count * 4 * width * streams * out_width,
    )


def taps_spectra(pieces, forward, me):
    groups = len(pieces)
    span, share = pieces[0].shape

    def kernel(at, *refs):
        piece_refs, (forward_ref, out_ref, padded) = refs[:groups], refs[groups:]
        row_ids = lax.broadcasted_iota(jnp.int32, (span, share), 0)
        for s in range(groups):
            k = lax.rem(at[0] - s + groups, groups)
            block = piece_refs[s][...]
            padded[0:span, pl.ds(pl.multiple_of(k * share, share), share)] = block

            @pl.when(k < groups - 1)
            def _():
                place = pl.multiple_of((k + 1) * share, share)
                kept = jnp.where(row_ids == 0, 0.0, block.astype(F32)).astype(BF16)
                padded[span : 2 * span, pl.ds(place, share)] = kept

        padded[span : 2 * span, 0:share] = jnp.zeros((span, share), BF16)
        out_ref[...] = dot(forward_ref[...], padded[...]).astype(BF16)

    shape = (2 * span, groups * share)
    return call(
        kernel,
        (1,),
        me[None],
        list(pieces) + [forward],
        [whole(p.shape) for p in pieces] + [whole(forward.shape)],
        jax.ShapeDtypeStruct(shape, BF16),
        whole(shape),
        [pltpu.VMEM(shape, BF16)],
        "taps_spectra",
        2 * shape[0] * shape[0] * shape[1],
        6 * shape[0] * shape[1],
    )


def long_filter(pieces, spectra_taps, forward_in, back, skip, me):
    groups = len(pieces)
    half, share = pieces[0][0].shape
    span = 2 * half
    cols = groups * share
    flat = [h for pair in pieces for h in pair]
    step = 16

    def kernel(at, *refs):
        ins, refs = refs[: 2 * groups], refs[2 * groups :]
        taps_ref, forward_ref, back_ref, skip_ref = refs[:4]
        outs, (signal, spectra, mixture, result) = refs[4 : 4 + 2 * groups], refs[4 + 2 * groups :]
        for s in range(groups):
            j = pl.multiple_of(lax.rem(at[0] - s + groups, groups) * share, share)
            signal[0:half, pl.ds(j, share)] = ins[2 * s][...]
            signal[half:span, pl.ds(j, share)] = ins[2 * s + 1][...]
        spectra[...] = dot(forward_ref[...], signal[...]).astype(BF16)

        def mix(start, special):
            def read(ref, first, block):
                return ref[pl.ds(first, step), block * share : (block + 1) * share].astype(F32)

            imag_start = start + span
            real_g = [read(taps_ref, start, b) for b in range(groups)]
            imag_g = [read(taps_ref, imag_start, b) for b in range(groups)]
            real_u = [read(spectra, start, b) for b in range(groups)]
            imag_u = [read(spectra, imag_start, b) for b in range(groups)]
            first = lax.broadcasted_iota(jnp.int32, (step, share), 0) == 0
            for i in range(groups):
                real = imag = None
                for j in range(i + 1):
                    rr = real_g[i - j] * real_u[j]
                    ii = imag_g[i - j] * imag_u[j]
                    cross = real_g[i - j] * imag_u[j] + imag_g[i - j] * real_u[j]
                    new_real, new_imag = rr - ii, cross
                    if special:
                        new_real = jnp.where(first, rr, new_real)
                        new_imag = jnp.where(first, ii, new_imag)
                    real = new_real if real is None else real + new_real
                    imag = new_imag if imag is None else imag + new_imag
                place = slice(i * share, (i + 1) * share)
                mixture[pl.ds(start, step), place] = real.astype(BF16)
                mixture[pl.ds(imag_start, step), place] = imag.astype(BF16)

        mix(0, True)

        @pl.loop(1, span // step)
        def _(c):
            mix(pl.multiple_of(c * step, step), False)

        result[...] = (
            dot(back_ref[...], mixture[...]) + skip_ref[...] * signal[...].astype(F32)
        ).astype(BF16)
        for s in range(groups):
            j = pl.multiple_of(lax.rem(at[0] + s, groups) * share, share)
            outs[2 * s][...] = result[0:half, pl.ds(j, share)]
            outs[2 * s + 1][...] = result[half:span, pl.ds(j, share)]

    operands = flat + [spectra_taps, forward_in, back, skip]
    outs = [jax.ShapeDtypeStruct(h.shape, BF16) for h in flat]
    found = call(
        kernel,
        (1,),
        me[None],
        operands,
        [whole(o.shape) for o in operands],
        outs,
        [whole(o.shape) for o in outs],
        [
            pltpu.VMEM((span, cols), BF16),
            pltpu.VMEM((2 * span, cols), BF16),
            pltpu.VMEM((2 * span, cols), BF16),
            pltpu.VMEM((span, cols), BF16),
        ],
        "long_filter",
        8 * span * span * cols,
        12 * span * cols,
    )
    return [(found[2 * s], found[2 * s + 1]) for s in range(groups)]


def gate_blocks(gate, pieces, me):
    groups = len(pieces)
    rows, share = pieces[0].shape

    def kernel(at, gate_ref, *refs):
        for s in range(groups):
            place = pl.multiple_of(lax.rem(at[0] - s + groups, groups) * share, share)
            gated = gate_ref[:, pl.ds(place, share)].astype(F32) * refs[s][...].astype(F32)
            refs[groups][:, pl.ds(place, share)] = gated.astype(BF16)

    return call(
        kernel,
        (1,),
        me[None],
        [gate] + list(pieces),
        [whole(gate.shape)] + [whole(p.shape) for p in pieces],
        jax.ShapeDtypeStruct(gate.shape, BF16),
        whole(gate.shape),
        [],
        "gate_blocks",
        rows * share * groups,
        6 * rows * share * groups,
    )


def output_shares(gated, other, w_own, w_other, chip_ids, core, kinds):
    count = len(chip_ids)
    rows, width = gated.shape
    cols = w_other.shape[1] * 2 // lax.axis_size("chan")

    def kernel(ids, a_ref, b_ref, w_ref, v_ref, *outs):
        k = pl.program_id(0)
        total = dot(a_ref[...], w_ref[...]) + dot(b_ref[...], v_ref[...])
        for j in range(count):

            @pl.when(k == j)
            def _():
                outs[j][...] = total.astype(kinds[j])

    outs = [jax.ShapeDtypeStruct((rows, cols), kind) for kind in kinds]
    return call(
        kernel,
        (count,),
        jnp.stack(list(chip_ids) + [core]).astype(jnp.int32),
        [gated, other, w_own, w_other],
        [
            whole(gated.shape),
            whole(other.shape),
            pl.BlockSpec((width, cols), lambda k, ids: (0, ids[k] * 2 + ids[count])),
            pl.BlockSpec((width, cols), lambda k, ids: (0, ids[k])),
        ],
        outs,
        [whole(o.shape) for o in outs],
        [],
        "output_shares",
        4 * count * rows * width * cols,
        4 * count * width * cols,
    )


def exchange(piece):
    return [piece(0)] + [shift(piece(s), "ctx", s) for s in range(1, lax.axis_size("ctx"))]


def in_order(blocks, me):
    groups = len(blocks)
    result = jnp.zeros((groups,) + blocks[0].shape, blocks[0].dtype)
    for s, b in enumerate(blocks):
        result = lax.dynamic_update_index_in_dim(result, b, (me - s) % groups, 0)
    return jnp.concatenate(list(result), 1)


def taps_spectra_plain(pieces, forward, me):
    groups = len(pieces)
    span, share = pieces[0].shape
    taps = in_order(pieces, me)
    before = jnp.concatenate(
        [jnp.zeros((span, share), BF16), taps[:, : (groups - 1) * share]], 1
    )
    before = jnp.where(lax.broadcasted_iota(jnp.int32, (span, 1), 0) == 0, 0, before)
    return dot(forward, jnp.concatenate([taps, before], 0)).astype(BF16)


def long_filter_plain(pieces, spectra_taps, forward_in, back, skip, me):
    groups = len(pieces)
    half, share = pieces[0][0].shape
    span = 2 * half
    signal = in_order([jnp.concatenate(pair, 0) for pair in pieces], me)
    spectra = dot(forward_in, signal).astype(BF16)
    real_g, imag_g = spectra_taps[:span].astype(F32), spectra_taps[span:].astype(F32)
    real_u, imag_u = spectra[:span].astype(F32), spectra[span:].astype(F32)
    first = lax.broadcasted_iota(jnp.int32, (span, 1), 0) == 0
    mixed = []
    for i in range(groups):
        real = imag = 0.0
        for j in range(i + 1):
            g = slice((i - j) * share, (i - j + 1) * share)
            u = slice(j * share, (j + 1) * share)
            rr = real_g[:, g] * real_u[:, u]
            ii = imag_g[:, g] * imag_u[:, u]
            cross = real_g[:, g] * imag_u[:, u] + imag_g[:, g] * real_u[:, u]
            real = real + jnp.where(first, rr, rr - ii)
            imag = imag + jnp.where(first, ii, cross)
        mixed.append(jnp.concatenate([real, imag], 0).astype(BF16))
    result = dot(back, jnp.concatenate(mixed, 1)) + skip * signal.astype(F32)
    result = jnp.stack(jnp.split(result.astype(BF16), groups, axis=1))
    found = []
    for s in range(groups):
        block = lax.dynamic_index_in_dim(result, (me + s) % groups, 0, keepdims=False)
        found.append((block[:half], block[half:]))
    return found


def gate_blocks_plain(gate, pieces, me):
    return (gate.astype(F32) * in_order(pieces, me).astype(F32)).astype(BF16)


def body(inputs, w_in, conv_taps, skip_gain, filter_taps, w_out):
    span, width = inputs.shape
    half = span // 2
    groups = lax.axis_size("ctx")
    me = lax.axis_index("ctx")
    chips = lax.axis_size("chan") // 2
    place = lax.axis_index("chan")
    chip, core = place // 2, place % 2
    share = width // groups
    aligned = share % 128 == 0
    out_width = w_out.shape[1] // (2 * chips)
    forward_np, back_np = half_tables(span)
    forward, back = jnp.asarray(forward_np), jnp.asarray(back_np)
    w_streams = jnp.transpose(w_in, (1, 0, 2))
    short_taps = conv_taps.reshape(-1, width).astype(F32)

    low = inputs[half - RIM :]
    rim = shift(inputs[span - RIM :], "ctx", 1)
    rim = jnp.where(me > 0, rim, jnp.zeros_like(rim))
    top = jnp.concatenate([rim, inputs[:half]], 0)

    low_found, top_found = [(0, low)], [(0, top)]
    low_up = low_down = low
    top_up = top_down = top
    for d in range(1, chips // 2 + 1):
        if 2 * d < chips:
            low_up = shift(low_up, "chan", 2)
            low_down = shift(low_down, "chan", -2)
            low_found += [(d, low_up), (-d, low_down)]
        else:
            low_far = shift(low_up, "chan", 2)
            low_found.append((d, low_far))
    top_down = after(top_down, low_down)
    top_up = after(top_up, low_far)
    for d in range(1, chips // 2 + 1):
        if 2 * d < chips:
            top_down = shift(top_down, "chan", -2)
            top_up = shift(top_up, "chan", 2)
            top_found += [(-d, top_down), (d, top_up)]
        else:
            top_found.append((-d, shift(top_down, "chan", -2)))

    split_taps = [filter_taps[:, q * share : (q + 1) * share] for q in range(groups)]
    split_taps = jnp.stack(split_taps)

    def pick(stack):
        return lambda s: lax.dynamic_index_in_dim(stack, (me + s) % groups, 0, keepdims=False)

    spectra_taps = (taps_spectra if aligned else taps_spectra_plain)(
        exchange(pick(split_taps)), forward, me
    )

    w_other = sibling(
        jnp.concatenate(
            [
                lax.dynamic_slice_in_dim(w_out, (2 * z + 1 - core) * out_width, out_width, 1)
                for z in range(chips)
            ],
            1,
        )
    )

    def stage(found, cut):
        pairs = [(block, sibling(block)) for _, block in found]
        ids = [(chip - d) % chips for d, _ in found]
        total = None
        if cut:
            (total,) = project(pairs[:cut], ids[:cut], core, w_streams, short_taps, groups)
        gate, gated = project(
            pairs[cut:], ids[cut:], core, w_streams, short_taps, groups, total, True
        )
        if not aligned:
            gated = jnp.stack(jnp.split(gated, groups, axis=1))
        return gate, exchange(pick(gated))

    gate_low, in_low = stage(low_found, 0)
    gate_top, in_top = stage(top_found, len(top_found) - 1)

    skip = lax.dynamic_slice_in_dim(skip_gain, me * share, share, 0)
    skip = jnp.tile(skip, groups)[None]
    filtered = (long_filter if aligned else long_filter_plain)(
        list(zip(in_top, in_low)), spectra_taps, forward[:, :span], back, skip, me
    )
    gating = gate_blocks if aligned else gate_blocks_plain
    gated_top = gating(gate_top, exchange(lambda s: filtered[s][0]), me)
    gated_low = gating(gate_low, exchange(lambda s: filtered[s][1]), me)

    def sums(gated, lead):
        other = sibling(gated)
        reach = chips // 2
        direct = [reach] + ([-lead * (reach - 1)] if reach > 1 else [])
        carried = [lead * d for d in range(reach - 1, 0, -1)]
        carried += [-lead * d for d in range(reach - 2, 0, -1)] + [0]

        def shares(offsets, kind):
            ids = [(chip + d) % chips for d in offsets]
            found = output_shares(gated, other, w_out, w_other, ids, core, [kind] * len(ids))
            return dict(zip(offsets, found))

        sent = shares(direct, BF16)
        kept = shares(carried, F32)
        ahead = shift(sent[reach], "chan", 2 * lead)
        behind = shift(sent[direct[1]], "chan", -2 * lead) if reach > 1 else None
        return ahead, behind, kept

    def finish(state, lead):
        ahead, behind, kept = state
        reach = chips // 2
        for d in range(reach - 1, 0, -1):
            ahead = shift((ahead.astype(F32) + kept[lead * d]).astype(BF16), "chan", 2 * lead)
        for d in range(reach - 2, 0, -1):
            behind = shift((behind.astype(F32) + kept[-lead * d]).astype(BF16), "chan", -2 * lead)
        total = kept[0] + ahead.astype(F32)
        if behind is not None:
            total = total + behind.astype(F32)
        return total.astype(BF16)

    state_top = sums(gated_top, 1)
    state_low = sums(gated_low, -1)
    return jnp.concatenate([finish(state_top, 1), finish(state_low, -1)], 0)


def solution(mesh):
    return jax.shard_map(
        body,
        mesh=mesh,
        in_specs=(
            P("ctx", "chan"),
            P(None, None, "chan"),
            P(None, None, "chan"),
            P("chan"),
            P("ctx", "chan"),
            P("chan", None),
        ),
        out_specs=P("ctx", "chan"),
        check_vma=False,
    )
```

```python
import math

import jax
import jax.numpy as jnp
import ml_dtypes
import numpy as np
from jax import lax
from jax.experimental import pallas as pl
from jax.experimental.pallas import tpu as pltpu
from jax.sharding import PartitionSpec as P

KERNEL = 3
RIM = 16
BF16 = jnp.bfloat16
F32 = jnp.float32
MIB = 1 << 20


def half_tables(span):
    n = 2 * span
    f = np.arange(span)[:, None]
    m = np.arange(n)[None, :]
    ang = 2.0 * math.pi * ((f * m) % n) / n
    real = np.cos(ang)
    imag = -np.sin(ang)
    imag[0] = np.where(np.arange(n) % 2 == 0, 1.0, -1.0)
    forward = np.concatenate([real, imag], 0).astype(ml_dtypes.bfloat16)
    weight = np.full((n, 1), 2.0 / n)
    weight[0] = 1.0 / n
    weight[span] = 1.0 / n
    back = (np.concatenate([real, imag], 0) * weight)[:, :span].T
    return forward, np.ascontiguousarray(back).astype(ml_dtypes.bfloat16)


def shift(x, axis, distance):
    size = lax.axis_size(axis)
    return lax.ppermute(x, axis, [(i, (i + distance) % size) for i in range(size)])


def sibling(x):
    return lax.ppermute(x, "chan", [(i, i ^ 1) for i in range(lax.axis_size("chan"))])


def dot(a, b):
    return jnp.dot(a, b, preferred_element_type=F32)


def after(x, *others):
    return lax.optimization_barrier((x,) + others)[0]


def whole(shape):
    return pl.BlockSpec(shape, lambda *_: (0,) * len(shape))


def call(kernel, grid, prefetch, operands, in_specs, outs, out_specs, scratch, name, flops, moved):
    return pl.pallas_call(
        kernel,
        grid_spec=pltpu.PrefetchScalarGridSpec(
            num_scalar_prefetch=1,
            grid=grid,
            in_specs=in_specs,
            out_specs=out_specs,
            scratch_shapes=scratch,
        ),
        out_shape=outs,
        compiler_params=pltpu.CompilerParams(vmem_limit_bytes=32 * MIB),
        cost_estimate=pl.CostEstimate(flops=flops, bytes_accessed=moved, transcendentals=0),
        name=name,
    )(prefetch, *operands)


def project(pairs, chip_ids, core, rim, w_in, conv_taps, groups, total=None, finish=False):
    count = len(pairs)
    parts = [p for pair in pairs for block in pair for p in block]
    span = sum(p.shape[0] for p in pairs[0][0])
    width = parts[0].shape[1]
    streams, _, out_width = w_in.shape
    rim_rows = rim.shape[0]
    rows = span + rim_rows
    split = out_width // groups % 128 == 0
    share = out_width // groups
    has_total = total is not None

    def kernel(ids, w_ref, rim_ref, *refs):
        part_refs, refs = refs[: len(parts)], refs[len(parts) :]
        if has_total:
            total_ref, refs = refs[0], refs[1:]
        if finish:
            taps_ref, gate_ref, in_ref, acc, x_own, x_other = refs
        else:
            acc, x_own, x_other = refs
        k, s = pl.program_id(0), pl.program_id(1)
        mine = pl.multiple_of(ids[count] * width, width)
        theirs = pl.multiple_of((1 - ids[count]) * width, width)
        at = 0
        for j in range(count):
            here = []
            for block in pairs[j]:
                here.append(part_refs[at : at + len(block)])
                at += len(block)

            @pl.when((k == j) & (s == 0))
            def _():
                for x, source, own in ((x_own, here[0], mine), (x_other, here[1], theirs)):
                    row = 0
                    for ref in source:
                        x[row : row + ref.shape[0]] = ref[...]
                        row += ref.shape[0]
                    first = pl.multiple_of(ids[j] * 2 * width + own, width)
                    x[span:rows] = rim_ref[:, pl.ds(first, width)]

        part = dot(x_own[...], w_ref[0, pl.ds(mine, width)])
        part = part + dot(x_other[...], w_ref[0, pl.ds(theirs, width)])
        if has_total:
            acc[s] = part + jnp.where(k == 0, total_ref[s], acc[s]) if count > 1 else part + total_ref[s]
        elif count == 1:
            acc[s] = part
        else:

            @pl.when(k == 0)
            def _():
                acc[s] = part

            @pl.when(k > 0)
            def _():
                acc[s] += part

        if finish:

            @pl.when((k == count - 1) & (s == streams - 1))
            def _():
                def filtered(t):
                    rounded = acc[t].astype(BF16).astype(F32)
                    longer = jnp.concatenate([rounded[rows - 8 :], rounded[:span]], 0)
                    result = jnp.zeros((span, out_width), F32)
                    for lag in range(KERNEL):
                        row = lag * streams + t
                        result = result + taps_ref[row : row + 1, :] * longer[8 - lag : 8 - lag + span]
                    return result.astype(BF16)

                gate_ref[...] = filtered(0)
                gated = (filtered(1).astype(F32) * filtered(2).astype(F32)).astype(BF16)
                if split:
                    for q in range(groups):
                        in_ref[q] = gated[:, q * share : (q + 1) * share]
                else:
                    in_ref[...] = gated

    in_specs = [pl.BlockSpec((1, 2 * width, out_width), lambda k, s, ids: (s, ids[k], 0))]
    in_specs += [whole(rim.shape)] + [whole(p.shape) for p in parts]
    operands = [w_in, rim] + parts
    if has_total:
        in_specs.append(whole(total.shape))
        operands.append(total)
    acc_shape = (streams, rows, out_width)
    scratch = [pltpu.VMEM((rows, width), BF16)] * 2
    if finish:
        in_specs.append(whole(conv_taps.shape))
        operands.append(conv_taps)
        in_shape = (groups, span, share) if split else (span, out_width)
        outs = [
            jax.ShapeDtypeStruct((span, out_width), BF16),
            jax.ShapeDtypeStruct(in_shape, BF16),
        ]
        scratch = [pltpu.VMEM(acc_shape, F32)] + scratch
    else:
        outs = [jax.ShapeDtypeStruct(acc_shape, F32)]
    return call(
        kernel,
        (count, streams),
        jnp.stack(list(chip_ids) + [core]).astype(jnp.int32),
        operands,
        in_specs,
        outs,
        [whole(o.shape) for o in outs],
        scratch,
        "project",
        4 * count * rows * width * streams * out_width,
        count * 4 * width * streams * out_width,
    )


def partner(me, slot, groups):
    if groups & (groups - 1) == 0:
        return me ^ slot
    return (me + slot) % groups


def source(me, slot, groups):
    if groups & (groups - 1) == 0:
        return me ^ slot
    return (me - slot + groups) % groups


def taps_spectra(pieces, forward, me):
    groups = len(pieces)
    span, share = pieces[0].shape

    def kernel(at, *refs):
        piece_refs, (forward_ref, out_ref, padded) = refs[:groups], refs[groups:]
        row_ids = lax.broadcasted_iota(jnp.int32, (span, share), 0)
        for s in range(groups):
            k = source(at[0], s, groups)
            block = piece_refs[s][...]
            padded[0:span, pl.ds(pl.multiple_of(k * share, share), share)] = block

            @pl.when(k < groups - 1)
            def _():
                place = pl.multiple_of((k + 1) * share, share)
                kept = jnp.where(row_ids == 0, 0.0, block.astype(F32)).astype(BF16)
                padded[span : 2 * span, pl.ds(place, share)] = kept

        padded[span : 2 * span, 0:share] = jnp.zeros((span, share), BF16)
        out_ref[...] = dot(forward_ref[...], padded[...]).astype(BF16)

    shape = (2 * span, groups * share)
    return call(
        kernel,
        (1,),
        me[None],
        list(pieces) + [forward],
        [whole(p.shape) for p in pieces] + [whole(forward.shape)],
        jax.ShapeDtypeStruct(shape, BF16),
        whole(shape),
        [pltpu.VMEM(shape, BF16)],
        "taps_spectra",
        2 * shape[0] * shape[0] * shape[1],
        6 * shape[0] * shape[1],
    )


def long_filter(pieces, spectra_taps, forward_in, back, skip, me):
    groups = len(pieces)
    span, share = pieces[0].shape
    half = span // 2
    cols = groups * share
    step = 16

    def kernel(at, *refs):
        ins, refs = refs[:groups], refs[groups:]
        taps_ref, forward_ref, back_ref, skip_ref = refs[:4]
        outs, (signal, spectra, mixture, result) = refs[4 : 4 + 2 * groups], refs[4 + 2 * groups :]
        for s in range(groups):
            j = pl.multiple_of(source(at[0], s, groups) * share, share)
            signal[:, pl.ds(j, share)] = ins[s][...]
        spectra[...] = dot(forward_ref[...], signal[...]).astype(BF16)

        def mix(start, special):
            def read(ref, first, block):
                return ref[pl.ds(first, step), block * share : (block + 1) * share].astype(F32)

            imag_start = start + span
            real_g = [read(taps_ref, start, b) for b in range(groups)]
            imag_g = [read(taps_ref, imag_start, b) for b in range(groups)]
            real_u = [read(spectra, start, b) for b in range(groups)]
            imag_u = [read(spectra, imag_start, b) for b in range(groups)]
            first = lax.broadcasted_iota(jnp.int32, (step, share), 0) == 0
            for i in range(groups):
                real = imag = None
                for j in range(i + 1):
                    rr = real_g[i - j] * real_u[j]
                    ii = imag_g[i - j] * imag_u[j]
                    cross = real_g[i - j] * imag_u[j] + imag_g[i - j] * real_u[j]
                    new_real, new_imag = rr - ii, cross
                    if special:
                        new_real = jnp.where(first, rr, new_real)
                        new_imag = jnp.where(first, ii, new_imag)
                    real = new_real if real is None else real + new_real
                    imag = new_imag if imag is None else imag + new_imag
                place = slice(i * share, (i + 1) * share)
                mixture[pl.ds(start, step), place] = real.astype(BF16)
                mixture[pl.ds(imag_start, step), place] = imag.astype(BF16)

        mix(0, True)

        @pl.loop(1, span // step)
        def _(c):
            mix(pl.multiple_of(c * step, step), False)

        result[...] = (
            dot(back_ref[...], mixture[...]) + skip_ref[...] * signal[...].astype(F32)
        ).astype(BF16)
        for s in range(groups):
            j = pl.multiple_of(partner(at[0], s, groups) * share, share)
            outs[2 * s][...] = result[0:half, pl.ds(j, share)]
            outs[2 * s + 1][...] = result[half:span, pl.ds(j, share)]

    operands = list(pieces) + [spectra_taps, forward_in, back, skip]
    outs = [jax.ShapeDtypeStruct((half, share), BF16)] * (2 * groups)
    found = call(
        kernel,
        (1,),
        me[None],
        operands,
        [whole(o.shape) for o in operands],
        outs,
        [whole(o.shape) for o in outs],
        [
            pltpu.VMEM((span, cols), BF16),
            pltpu.VMEM((2 * span, cols), BF16),
            pltpu.VMEM((2 * span, cols), BF16),
            pltpu.VMEM((span, cols), BF16),
        ],
        "long_filter",
        8 * span * span * cols,
        12 * span * cols,
    )
    return [(found[2 * s], found[2 * s + 1]) for s in range(groups)]


def gate_blocks(gate, pieces, me):
    groups = len(pieces)
    rows, share = pieces[0].shape

    def kernel(at, gate_ref, *refs):
        for s in range(groups):
            place = pl.multiple_of(source(at[0], s, groups) * share, share)
            gated = gate_ref[:, pl.ds(place, share)].astype(F32) * refs[s][...].astype(F32)
            refs[groups][:, pl.ds(place, share)] = gated.astype(BF16)

    return call(
        kernel,
        (1,),
        me[None],
        [gate] + list(pieces),
        [whole(gate.shape)] + [whole(p.shape) for p in pieces],
        jax.ShapeDtypeStruct(gate.shape, BF16),
        whole(gate.shape),
        [],
        "gate_blocks",
        rows * share * groups,
        6 * rows * share * groups,
    )


def output_shares(gated, other, w_own, w_other, chip_ids, core, kinds):
    count = len(chip_ids)
    rows, width = gated.shape
    cols = w_other.shape[1] * 2 // lax.axis_size("chan")

    def kernel(ids, a_ref, b_ref, w_ref, v_ref, *outs):
        k = pl.program_id(0)
        total = dot(a_ref[...], w_ref[...]) + dot(b_ref[...], v_ref[...])
        for j in range(count):

            @pl.when(k == j)
            def _():
                outs[j][...] = total.astype(kinds[j])

    outs = [jax.ShapeDtypeStruct((rows, cols), kind) for kind in kinds]
    return call(
        kernel,
        (count,),
        jnp.stack(list(chip_ids) + [core]).astype(jnp.int32),
        [gated, other, w_own, w_other],
        [
            whole(gated.shape),
            whole(other.shape),
            pl.BlockSpec((width, cols), lambda k, ids: (0, ids[k] * 2 + ids[count])),
            pl.BlockSpec((width, cols), lambda k, ids: (0, ids[k])),
        ],
        outs,
        [whole(o.shape) for o in outs],
        [],
        "output_shares",
        4 * count * rows * width * cols,
        4 * count * width * cols,
    )


def exchange(piece):
    groups = lax.axis_size("ctx")

    def send(slot):
        route = [(i, partner(i, slot, groups)) for i in range(groups)]
        return lax.ppermute(piece(slot), "ctx", route)

    return [piece(0)] + [send(s) for s in range(1, groups)]


def in_order(blocks, me):
    groups = len(blocks)
    result = jnp.zeros((groups,) + blocks[0].shape, blocks[0].dtype)
    for s, b in enumerate(blocks):
        result = lax.dynamic_update_index_in_dim(result, b, source(me, s, groups), 0)
    return jnp.concatenate(list(result), 1)


def taps_spectra_plain(pieces, forward, me):
    groups = len(pieces)
    span, share = pieces[0].shape
    taps = in_order(pieces, me)
    before = jnp.concatenate(
        [jnp.zeros((span, share), BF16), taps[:, : (groups - 1) * share]], 1
    )
    before = jnp.where(lax.broadcasted_iota(jnp.int32, (span, 1), 0) == 0, 0, before)
    return dot(forward, jnp.concatenate([taps, before], 0)).astype(BF16)


def long_filter_plain(pieces, spectra_taps, forward_in, back, skip, me):
    groups = len(pieces)
    span, share = pieces[0].shape
    half = span // 2
    signal = in_order(pieces, me)
    spectra = dot(forward_in, signal).astype(BF16)
    real_g, imag_g = spectra_taps[:span].astype(F32), spectra_taps[span:].astype(F32)
    real_u, imag_u = spectra[:span].astype(F32), spectra[span:].astype(F32)
    first = lax.broadcasted_iota(jnp.int32, (span, 1), 0) == 0
    mixed = []
    for i in range(groups):
        real = imag = 0.0
        for j in range(i + 1):
            g = slice((i - j) * share, (i - j + 1) * share)
            u = slice(j * share, (j + 1) * share)
            rr = real_g[:, g] * real_u[:, u]
            ii = imag_g[:, g] * imag_u[:, u]
            cross = real_g[:, g] * imag_u[:, u] + imag_g[:, g] * real_u[:, u]
            real = real + jnp.where(first, rr, rr - ii)
            imag = imag + jnp.where(first, ii, cross)
        mixed.append(jnp.concatenate([real, imag], 0).astype(BF16))
    result = dot(back, jnp.concatenate(mixed, 1)) + skip * signal.astype(F32)
    result = jnp.stack(jnp.split(result.astype(BF16), groups, axis=1))
    found = []
    for s in range(groups):
        block = lax.dynamic_index_in_dim(result, partner(me, s, groups), 0, keepdims=False)
        found.append((block[:half], block[half:]))
    return found


def gate_blocks_plain(gate, pieces, me):
    return (gate.astype(F32) * in_order(pieces, me).astype(F32)).astype(BF16)


def body(inputs, w_in, conv_taps, skip_gain, filter_taps, w_out):
    span, width = inputs.shape
    half = span // 2
    groups = lax.axis_size("ctx")
    me = lax.axis_index("ctx")
    chips = lax.axis_size("chan") // 2
    place = lax.axis_index("chan")
    chip, core = place // 2, place % 2
    share = width // groups
    aligned = share % 128 == 0
    out_width = w_out.shape[1] // (2 * chips)
    forward_np, back_np = half_tables(span)
    forward, back = jnp.asarray(forward_np), jnp.asarray(back_np)
    w_streams = jnp.transpose(w_in, (1, 0, 2))
    short_taps = conv_taps.reshape(-1, width).astype(F32)

    found = [(0, [inputs])]
    up = down = inputs
    for d in range(1, chips // 2 + 1):
        if 2 * d < chips:
            up, down = shift(up, "chan", 2), shift(down, "chan", -2)
            found += [(d, [up]), (-d, [down])]
        else:
            far = [shift(up[:half], "chan", 2), shift(down[half:], "chan", -2)]
            found.append((d, far))

    rim = shift(inputs[span - RIM :], "ctx", 1)
    rim = jnp.where(me > 0, rim, jnp.zeros_like(rim))
    rim = lax.all_gather(rim, "chan", axis=1, tiled=True)

    split_taps = [filter_taps[:, q * share : (q + 1) * share] for q in range(groups)]
    split_taps = jnp.stack(split_taps)

    def pick(stack):
        return lambda s: lax.dynamic_index_in_dim(
            stack, partner(me, s, groups), 0, keepdims=False
        )

    spectra_taps = (taps_spectra if aligned else taps_spectra_plain)(
        exchange(pick(split_taps)), forward, me
    )

    w_other = sibling(
        jnp.concatenate(
            [
                lax.dynamic_slice_in_dim(w_out, (2 * z + 1 - core) * out_width, out_width, 1)
                for z in range(chips)
            ],
            1,
        )
    )

    rim = after(rim, spectra_taps)
    pairs = [(block, [sibling(p) for p in block]) for _, block in found]
    ids = [(chip - d) % chips for d, _ in found]
    (total,) = project(pairs[:-1], ids[:-1], core, rim, w_streams, short_taps, groups)
    gate, gated = project(
        pairs[-1:], ids[-1:], core, rim, w_streams, short_taps, groups, total, True
    )
    if not aligned:
        gated = jnp.stack(jnp.split(gated, groups, axis=1))

    skip = lax.dynamic_slice_in_dim(skip_gain, me * share, share, 0)
    skip = jnp.tile(skip, groups)[None]
    filtered = (long_filter if aligned else long_filter_plain)(
        exchange(pick(gated)), spectra_taps, forward[:, :span], back, skip, me
    )
    gating = gate_blocks if aligned else gate_blocks_plain
    gated_top = gating(gate[:half], exchange(lambda s: filtered[s][0]), me)

    def sums(gated, lead):
        other = sibling(gated)
        reach = chips // 2
        direct = [reach] + ([-lead * (reach - 1)] if reach > 1 else [])
        carried = [lead * d for d in range(reach - 1, 0, -1)]
        carried += [-lead * d for d in range(reach - 2, 0, -1)] + [0]

        def shares(offsets, kind):
            ids = [(chip + d) % chips for d in offsets]
            found = output_shares(gated, other, w_out, w_other, ids, core, [kind] * len(ids))
            return dict(zip(offsets, found))

        sent = shares(direct, BF16)
        kept = shares(carried, F32)
        ahead = shift(sent[reach], "chan", 2 * lead)
        behind = shift(sent[direct[1]], "chan", -2 * lead) if reach > 1 else None
        return ahead, behind, kept, sent[reach]

    def finish(state, lead):
        ahead, behind, kept, _ = state
        reach = chips // 2
        for d in range(reach - 1, 0, -1):
            ahead = shift((ahead.astype(F32) + kept[lead * d]).astype(BF16), "chan", 2 * lead)
        for d in range(reach - 2, 0, -1):
            behind = shift((behind.astype(F32) + kept[-lead * d]).astype(BF16), "chan", -2 * lead)
        total = kept[0] + ahead.astype(F32)
        if behind is not None:
            total = total + behind.astype(F32)
        return total.astype(BF16)

    state_top = sums(gated_top, 1)
    low = [after(f[1], state_top[3]) for f in filtered]
    gated_low = gating(gate[half:], exchange(lambda s: low[s]), me)
    state_low = sums(gated_low, -1)
    return jnp.concatenate([finish(state_top, 1), finish(state_low, -1)], 0)


def solution(mesh):
    return jax.shard_map(
        body,
        mesh=mesh,
        in_specs=(
            P("ctx", "chan"),
            P(None, None, "chan"),
            P(None, None, "chan"),
            P("chan"),
            P("ctx", "chan"),
            P("chan", None),
        ),
        out_specs=P("ctx", "chan"),
        check_vma=False,
    )
```

```python
import math

import jax
import jax.numpy as jnp
import ml_dtypes
import numpy as np
from jax import lax
from jax.experimental import pallas as pl
from jax.experimental.pallas import tpu as pltpu
from jax.sharding import PartitionSpec as P

KERNEL = 3
RIM = 16
BF16 = jnp.bfloat16
F32 = jnp.float32
MIB = 1 << 20


def half_tables(span):
    n = 2 * span
    f = np.arange(span)[:, None]
    m = np.arange(n)[None, :]
    ang = 2.0 * math.pi * ((f * m) % n) / n
    real = np.cos(ang)
    imag = -np.sin(ang)
    imag[0] = np.where(np.arange(n) % 2 == 0, 1.0, -1.0)
    forward = np.concatenate([real, imag], 0).astype(ml_dtypes.bfloat16)
    weight = np.full((n, 1), 2.0 / n)
    weight[0] = 1.0 / n
    weight[span] = 1.0 / n
    back = (np.concatenate([real, imag], 0) * weight)[:, :span].T
    return forward, np.ascontiguousarray(back).astype(ml_dtypes.bfloat16)


def shift(x, axis, distance):
    size = lax.axis_size(axis)
    return lax.ppermute(x, axis, [(i, (i + distance) % size) for i in range(size)])


def sibling(x):
    return lax.ppermute(x, "chan", [(i, i ^ 1) for i in range(lax.axis_size("chan"))])


def dot(a, b):
    return jnp.dot(a, b, preferred_element_type=F32)


def after(x, *others):
    return lax.optimization_barrier((x,) + others)[0]


def in_hbm(x):
    return pltpu.with_memory_space_constraint(x, pltpu.HBM)


def whole(shape):
    return pl.BlockSpec(shape, lambda *_: (0,) * len(shape))


def call(kernel, grid, prefetch, operands, in_specs, outs, out_specs, scratch, name, micros=1):
    return pl.pallas_call(
        kernel,
        grid_spec=pltpu.PrefetchScalarGridSpec(
            num_scalar_prefetch=1,
            grid=grid,
            in_specs=in_specs,
            out_specs=out_specs,
            scratch_shapes=scratch,
        ),
        out_shape=outs,
        compiler_params=pltpu.CompilerParams(vmem_limit_bytes=32 * MIB),
        cost_estimate=pl.CostEstimate(
            flops=micros * 10**9, bytes_accessed=micros << 20, transcendentals=0
        ),
        name=name,
    )(prefetch, *operands)


def project(pairs, chip_ids, slots, core, rims, w_in, conv_taps, groups, total=None, finish=False):
    count = len(pairs)
    parts = [p for pair in pairs for block in pair for p in block]
    span = sum(p.shape[0] for p in pairs[0][0])
    width = parts[0].shape[1]
    streams, _, out_width = w_in.shape
    rim_rows = RIM
    rows = span + rim_rows
    split = out_width // groups % 128 == 0
    share = out_width // groups
    has_total = total is not None

    def kernel(ids, w_ref, rim_own, rim_other, *refs):
        part_refs, refs = refs[: len(parts)], refs[len(parts) :]
        if has_total:
            total_ref, refs = refs[0], refs[1:]
        if finish:
            taps_ref, gate_ref, in_ref, acc, x_own, x_other = refs
        else:
            acc, x_own, x_other = refs
        k, s = pl.program_id(0), pl.program_id(1)
        mine = pl.multiple_of(ids[count] * width, width)
        theirs = pl.multiple_of((1 - ids[count]) * width, width)
        at = 0
        for j in range(count):
            here = []
            for block in pairs[j]:
                here.append(part_refs[at : at + len(block)])
                at += len(block)

            @pl.when((k == j) & (s == 0))
            def _():
                for x, source, rim in ((x_own, here[0], rim_own), (x_other, here[1], rim_other)):
                    row = 0
                    for ref in source:
                        x[row : row + ref.shape[0]] = ref[...]
                        row += ref.shape[0]
                    x[span:rows] = rim[slots[j] * RIM : (slots[j] + 1) * RIM]

        part = dot(x_own[...], w_ref[0, pl.ds(mine, width)])
        part = part + dot(x_other[...], w_ref[0, pl.ds(theirs, width)])
        if has_total:
            acc[s] = part + jnp.where(k == 0, total_ref[s], acc[s]) if count > 1 else part + total_ref[s]
        elif count == 1:
            acc[s] = part
        else:

            @pl.when(k == 0)
            def _():
                acc[s] = part

            @pl.when(k > 0)
            def _():
                acc[s] += part

        if finish:

            @pl.when((k == count - 1) & (s == streams - 1))
            def _():
                def filtered(t):
                    rounded = acc[t].astype(BF16).astype(F32)
                    longer = jnp.concatenate([rounded[rows - 8 :], rounded[:span]], 0)
                    result = jnp.zeros((span, out_width), F32)
                    for lag in range(KERNEL):
                        row = lag * streams + t
                        result = result + taps_ref[row : row + 1, :] * longer[8 - lag : 8 - lag + span]
                    return result.astype(BF16)

                gate_ref[...] = filtered(0)
                gated = (filtered(1).astype(F32) * filtered(2).astype(F32)).astype(BF16)
                if split:
                    for q in range(groups):
                        in_ref[q] = gated[:, q * share : (q + 1) * share]
                else:
                    in_ref[...] = gated

    in_specs = [pl.BlockSpec((1, 2 * width, out_width), lambda k, s, ids: (s, ids[k], 0))]
    in_specs += [whole(r.shape) for r in rims] + [whole(p.shape) for p in parts]
    operands = [in_hbm(w_in)] + list(rims) + parts
    if has_total:
        in_specs.append(whole(total.shape))
        operands.append(total)
    acc_shape = (streams, rows, out_width)
    scratch = [pltpu.VMEM((rows, width), BF16)] * 2
    if finish:
        in_specs.append(whole(conv_taps.shape))
        operands.append(conv_taps)
        in_shape = (groups, span, share) if split else (span, out_width)
        outs = [
            jax.ShapeDtypeStruct((span, out_width), BF16),
            jax.ShapeDtypeStruct(in_shape, BF16),
        ]
        scratch = [pltpu.VMEM(acc_shape, F32)] + scratch
    else:
        outs = [jax.ShapeDtypeStruct(acc_shape, F32)]
    return call(
        kernel,
        (count, streams),
        jnp.stack(list(chip_ids) + [core]).astype(jnp.int32),
        operands,
        in_specs,
        outs,
        [whole(o.shape) for o in outs],
        scratch,
        "project",
        20 if count > 1 else 4,
    )


def partner(me, slot, groups):
    if groups & (groups - 1) == 0:
        return me ^ slot
    return (me + slot) % groups


def source(me, slot, groups):
    if groups & (groups - 1) == 0:
        return me ^ slot
    return (me - slot + groups) % groups


def taps_spectra(pieces, forward, me):
    groups = len(pieces)
    span, share = pieces[0].shape

    def kernel(at, *refs):
        piece_refs, (forward_ref, out_ref, padded) = refs[:groups], refs[groups:]
        row_ids = lax.broadcasted_iota(jnp.int32, (span, share), 0)
        for s in range(groups):
            k = source(at[0], s, groups)
            block = piece_refs[s][...]
            padded[0:span, pl.ds(pl.multiple_of(k * share, share), share)] = block

            @pl.when(k < groups - 1)
            def _():
                place = pl.multiple_of((k + 1) * share, share)
                kept = jnp.where(row_ids == 0, 0.0, block.astype(F32)).astype(BF16)
                padded[span : 2 * span, pl.ds(place, share)] = kept

        padded[span : 2 * span, 0:share] = jnp.zeros((span, share), BF16)
        out_ref[...] = dot(forward_ref[...], padded[...]).astype(BF16)

    shape = (2 * span, groups * share)
    return call(
        kernel,
        (1,),
        me[None],
        list(pieces) + [in_hbm(forward)],
        [whole(p.shape) for p in pieces] + [whole(forward.shape)],
        jax.ShapeDtypeStruct(shape, BF16),
        whole(shape),
        [pltpu.VMEM(shape, BF16)],
        "taps_spectra",
        2,
    )


def long_filter(pieces, spectra_taps, forward_in, back, skip, me):
    groups = len(pieces)
    span, share = pieces[0].shape
    cols = groups * share
    step = 16

    def kernel(at, *refs):
        ins, refs = refs[:groups], refs[groups:]
        taps_ref, forward_ref, back_ref, skip_ref = refs[:4]
        outs, refs = refs[4 : 4 + groups], refs[4 + groups :]
        signal, spectra, mixture, result, forward_own, back_own, ready = refs
        tables = ((forward_ref, forward_own), (back_ref, back_own))
        copies = [
            pltpu.make_async_copy(far, near, ready.at[k]) for k, (far, near) in enumerate(tables)
        ]
        for copy in copies:
            copy.start()
        for s in range(groups):
            j = pl.multiple_of(source(at[0], s, groups) * share, share)
            signal[:, pl.ds(j, share)] = ins[s][...]
        copies[0].wait()
        spectra[...] = dot(forward_own[...], signal[...]).astype(BF16)

        def mix(start, special):
            def read(ref, first, block):
                return ref[pl.ds(first, step), block * share : (block + 1) * share].astype(F32)

            imag_start = start + span
            real_g = [read(taps_ref, start, b) for b in range(groups)]
            imag_g = [read(taps_ref, imag_start, b) for b in range(groups)]
            real_u = [read(spectra, start, b) for b in range(groups)]
            imag_u = [read(spectra, imag_start, b) for b in range(groups)]
            first = lax.broadcasted_iota(jnp.int32, (step, share), 0) == 0
            for i in range(groups):
                real = imag = None
                for j in range(i + 1):
                    rr = real_g[i - j] * real_u[j]
                    ii = imag_g[i - j] * imag_u[j]
                    cross = real_g[i - j] * imag_u[j] + imag_g[i - j] * real_u[j]
                    new_real, new_imag = rr - ii, cross
                    if special:
                        new_real = jnp.where(first, rr, new_real)
                        new_imag = jnp.where(first, ii, new_imag)
                    real = new_real if real is None else real + new_real
                    imag = new_imag if imag is None else imag + new_imag
                place = slice(i * share, (i + 1) * share)
                mixture[pl.ds(start, step), place] = real.astype(BF16)
                mixture[pl.ds(imag_start, step), place] = imag.astype(BF16)

        mix(0, True)

        @pl.loop(1, span // step)
        def _(c):
            mix(pl.multiple_of(c * step, step), False)

        copies[1].wait()
        result[...] = (
            dot(back_own[...], mixture[...]) + skip_ref[...] * signal[...].astype(F32)
        ).astype(BF16)
        for s in range(groups):
            j = pl.multiple_of(partner(at[0], s, groups) * share, share)
            outs[s][...] = result[:, pl.ds(j, share)]

    operands = list(pieces) + [spectra_taps, in_hbm(forward_in), in_hbm(back), skip]
    in_specs = [whole(o.shape) for o in operands]
    in_specs[groups + 1] = in_specs[groups + 2] = pl.BlockSpec(memory_space=pltpu.HBM)
    outs = [jax.ShapeDtypeStruct((span, share), BF16)] * groups
    return call(
        kernel,
        (1,),
        me[None],
        operands,
        in_specs,
        outs,
        [whole(o.shape) for o in outs],
        [
            pltpu.VMEM((span, cols), BF16),
            pltpu.VMEM((2 * span, cols), BF16),
            pltpu.VMEM((2 * span, cols), BF16),
            pltpu.VMEM((span, cols), BF16),
            pltpu.VMEM(forward_in.shape, BF16),
            pltpu.VMEM(back.shape, BF16),
            pltpu.SemaphoreType.DMA((2,)),
        ],
        "long_filter",
        3,
    )


def gate_blocks(gate, pieces, me):
    groups = len(pieces)
    rows, share = pieces[0].shape

    def kernel(at, gate_ref, *refs):
        for s in range(groups):
            place = pl.multiple_of(source(at[0], s, groups) * share, share)
            gated = gate_ref[:, pl.ds(place, share)].astype(F32) * refs[s][...].astype(F32)
            refs[groups][:, pl.ds(place, share)] = gated.astype(BF16)

    return call(
        kernel,
        (1,),
        me[None],
        [gate] + list(pieces),
        [whole(gate.shape)] + [whole(p.shape) for p in pieces],
        jax.ShapeDtypeStruct(gate.shape, BF16),
        whole(gate.shape),
        [],
        "gate_blocks",
    )


def output_shares(gated, other, w_own, w_other, chip_ids, core, plan):
    count = len(chip_ids)
    rows, width = gated.shape
    cols = w_other.shape[1] * 2 // lax.axis_size("chan")

    def kernel(ids, a_ref, b_ref, w_ref, v_ref, *outs):
        k = pl.program_id(0)
        total = dot(a_ref[...], w_ref[...]) + dot(b_ref[...], v_ref[...])
        at = 0
        for j in range(count):
            here = outs[at : at + len(plan[j])]
            at += len(plan[j])

            @pl.when(k == j)
            def _():
                for out, (first, last, kind) in zip(here, plan[j]):
                    out[...] = total[first:last].astype(kind)

    outs = [
        jax.ShapeDtypeStruct((last - first, cols), kind)
        for parts in plan
        for first, last, kind in parts
    ]
    return call(
        kernel,
        (count,),
        jnp.stack(list(chip_ids) + [core]).astype(jnp.int32),
        [gated, other, in_hbm(w_own), w_other],
        [
            whole(gated.shape),
            whole(other.shape),
            pl.BlockSpec((width, cols), lambda k, ids: (0, ids[k] * 2 + ids[count])),
            pl.BlockSpec((width, cols), lambda k, ids: (0, ids[k])),
        ],
        outs,
        [whole(o.shape) for o in outs],
        [],
        "output_shares",
    )


def add_up(own, extras):
    span, cols = own.shape
    half = span // 2
    flat = [e for side in extras for e in side]

    def kernel(_, own_ref, *refs):
        at = 0
        for k, side in enumerate(extras):
            total = own_ref[k * half : (k + 1) * half]
            for ref in refs[at : at + len(side)]:
                total = total + ref[...].astype(F32)
            at += len(side)
            refs[-1][k * half : (k + 1) * half] = total.astype(BF16)

    return call(
        kernel,
        (1,),
        jnp.zeros((1,), jnp.int32),
        [own] + flat,
        [whole(own.shape)] + [whole(e.shape) for e in flat],
        jax.ShapeDtypeStruct(own.shape, BF16),
        whole(own.shape),
        [],
        "add_up",
    )


def exchange(piece):
    groups = lax.axis_size("ctx")

    def send(slot):
        route = [(i, partner(i, slot, groups)) for i in range(groups)]
        return lax.ppermute(piece(slot), "ctx", route)

    return [piece(0)] + [send(s) for s in range(1, groups)]


def in_order(blocks, me):
    groups = len(blocks)
    result = jnp.zeros((groups,) + blocks[0].shape, blocks[0].dtype)
    for s, b in enumerate(blocks):
        result = lax.dynamic_update_index_in_dim(result, b, source(me, s, groups), 0)
    return jnp.concatenate(list(result), 1)


def taps_spectra_plain(pieces, forward, me):
    groups = len(pieces)
    span, share = pieces[0].shape
    taps = in_order(pieces, me)
    before = jnp.concatenate(
        [jnp.zeros((span, share), BF16), taps[:, : (groups - 1) * share]], 1
    )
    before = jnp.where(lax.broadcasted_iota(jnp.int32, (span, 1), 0) == 0, 0, before)
    return dot(forward, jnp.concatenate([taps, before], 0)).astype(BF16)


def long_filter_plain(pieces, spectra_taps, forward_in, back, skip, me):
    groups = len(pieces)
    span, share = pieces[0].shape
    signal = in_order(pieces, me)
    spectra = dot(forward_in, signal).astype(BF16)
    real_g, imag_g = spectra_taps[:span].astype(F32), spectra_taps[span:].astype(F32)
    real_u, imag_u = spectra[:span].astype(F32), spectra[span:].astype(F32)
    first = lax.broadcasted_iota(jnp.int32, (span, 1), 0) == 0
    mixed = []
    for i in range(groups):
        real = imag = 0.0
        for j in range(i + 1):
            g = slice((i - j) * share, (i - j + 1) * share)
            u = slice(j * share, (j + 1) * share)
            rr = real_g[:, g] * real_u[:, u]
            ii = imag_g[:, g] * imag_u[:, u]
            cross = real_g[:, g] * imag_u[:, u] + imag_g[:, g] * real_u[:, u]
            real = real + jnp.where(first, rr, rr - ii)
            imag = imag + jnp.where(first, ii, cross)
        mixed.append(jnp.concatenate([real, imag], 0).astype(BF16))
    result = dot(back, jnp.concatenate(mixed, 1)) + skip * signal.astype(F32)
    result = jnp.stack(jnp.split(result.astype(BF16), groups, axis=1))
    found = []
    for s in range(groups):
        block = lax.dynamic_index_in_dim(result, partner(me, s, groups), 0, keepdims=False)
        found.append(block)
    return found


def gate_blocks_plain(gate, pieces, me):
    return (gate.astype(F32) * in_order(pieces, me).astype(F32)).astype(BF16)


def body(inputs, w_in, conv_taps, skip_gain, filter_taps, w_out):
    span, width = inputs.shape
    half = span // 2
    groups = lax.axis_size("ctx")
    me = lax.axis_index("ctx")
    chips = lax.axis_size("chan") // 2
    reach = chips // 2
    place = lax.axis_index("chan")
    chip, core = place // 2, place % 2
    share = width // groups
    aligned = share % 128 == 0
    out_width = w_out.shape[1] // (2 * chips)
    forward_np, back_np = half_tables(span)
    forward, back = jnp.asarray(forward_np), jnp.asarray(back_np)
    forward_in = jnp.asarray(np.ascontiguousarray(forward_np[:, :span]))
    w_streams = jnp.transpose(w_in, (1, 0, 2))
    short_taps = conv_taps.reshape(-1, width).astype(F32)

    rim = shift(inputs[span - RIM :], "ctx", 1)
    rim = jnp.where(me > 0, rim, jnp.zeros_like(rim))
    rim = jnp.concatenate([rim] + [shift(rim, "chan", 2 * s) for s in range(1, chips)], 0)
    rims = (rim, sibling(rim))

    split_taps = [filter_taps[:, q * share : (q + 1) * share] for q in range(groups)]
    split_taps = jnp.stack(split_taps)

    def pick(stack):
        return lambda s: lax.dynamic_index_in_dim(
            stack, partner(me, s, groups), 0, keepdims=False
        )

    tap_blocks = exchange(pick(split_taps))

    w_given = jnp.concatenate(
        [
            lax.dynamic_slice_in_dim(w_out, (2 * z + 1 - core) * out_width, out_width, 1)
            for z in range(chips)
        ],
        1,
    )

    found = [(0, [inputs])]
    up = down = inputs
    for d in range(1, chips // 2 + 1):
        if 2 * d < chips:
            up, down = shift(up, "chan", 2), shift(down, "chan", -2)
            if d == 1:
                up, down, rims, tap_blocks, w_given = lax.optimization_barrier(
                    (up, down, rims, tap_blocks, w_given)
                )
            found += [(d, [up]), (-d, [down])]
        else:
            far = [shift(up[:half], "chan", 2), shift(down[half:], "chan", -2)]
    spectra_taps = (taps_spectra if aligned else taps_spectra_plain)(tap_blocks, forward, me)

    def both(blocks):
        return blocks, [sibling(b) for b in blocks]

    def added(blocks, total=None):
        return project(
            [both(b) for _, b in blocks],
            [(chip - d) % chips for d, _ in blocks],
            [d % chips for d, _ in blocks],
            core,
            rims,
            w_streams,
            short_taps,
            groups,
            total,
            total is not None,
        )

    (total,) = added(found)
    far = [after(f, total) for f in far]
    gate, gated = added([(reach, far)], total)
    if not aligned:
        gated = jnp.stack(jnp.split(gated, groups, axis=1))

    w_other = sibling(after(w_given, gated))

    skip = lax.dynamic_slice_in_dim(skip_gain, me * share, share, 0)
    skip = jnp.tile(skip, groups)[None]
    filtered = (long_filter if aligned else long_filter_plain)(
        exchange(pick(gated)), spectra_taps, forward_in, back, skip, me
    )
    filtered = lax.optimization_barrier((list(filtered), w_other))[0]
    gated_out = (gate_blocks if aligned else gate_blocks_plain)(
        gate, exchange(lambda s: filtered[s]), me
    )

    other = sibling(gated_out)

    def shares(offsets, plan):
        ids = [(chip + d) % chips for d in offsets]
        return output_shares(gated_out, other, w_out, w_other, ids, core, plan)

    up_top, down_low = shares([reach], [[(0, half, BF16), (half, span, BF16)]])
    offsets, plan = [], []
    for d in range(reach - 1, 0, -1):
        last = d == reach - 1
        offsets += [d, -d]
        plan.append([(0, half, F32), (half, span, BF16 if last else F32)])
        plan.append([(0, half, BF16 if last else F32), (half, span, F32)])
    kept = list(shares(offsets + [0], plan + [[(0, span, F32)]]))
    up_top, down_low = shift(up_top, "chan", 2), shift(down_low, "chan", -2)
    up_low = down_top = None

    def step(carried, new, distance):
        if carried is not None:
            new = (carried.astype(F32) + new).astype(BF16)
        return shift(new, "chan", distance)

    for k in range(reach - 1):
        ahead_top, ahead_low, behind_top, behind_low = kept[4 * k : 4 * k + 4]
        up_low, down_top = step(up_low, ahead_low, 2), step(down_top, behind_top, -2)
        up_top, down_low = step(up_top, ahead_top, 2), step(down_low, behind_low, -2)
    extras = [[up_top], [down_low]]
    if reach > 1:
        extras = [[up_top, down_top], [up_low, down_low]]
    return add_up(kept[-1], extras)


def solution(mesh):
    return jax.shard_map(
        body,
        mesh=mesh,
        in_specs=(
            P("ctx", "chan"),
            P(None, None, "chan"),
            P(None, None, "chan"),
            P("chan"),
            P("ctx", "chan"),
            P("chan", None),
        ),
        out_specs=P("ctx", "chan"),
        check_vma=False,
    )
```

```python
import math

import jax
import jax.numpy as jnp
import ml_dtypes
import numpy as np
from jax import lax
from jax.experimental import pallas as pl
from jax.experimental.pallas import tpu as pltpu
from jax.sharding import PartitionSpec as P

KERNEL = 3
EDGE = 16
BF16 = jnp.bfloat16
F32 = jnp.float32
MIB = 1 << 20


def half_tables(span):
    n = 2 * span
    f = np.arange(span)[:, None]
    m = np.arange(n)[None, :]
    ang = 2.0 * math.pi * ((f * m) % n) / n
    real = np.cos(ang)
    imag = -np.sin(ang)
    imag[0] = np.where(np.arange(n) % 2 == 0, 1.0, -1.0)
    forward = np.concatenate([real, imag], 0).astype(ml_dtypes.bfloat16)
    weight = np.full((n, 1), 2.0 / n)
    weight[0] = 1.0 / n
    weight[span] = 1.0 / n
    back = (np.concatenate([real, imag], 0) * weight)[:, :span].T
    return forward, np.ascontiguousarray(back).astype(ml_dtypes.bfloat16)


def shift(x, axis, distance):
    size = lax.axis_size(axis)
    return lax.ppermute(x, axis, [(i, (i + distance) % size) for i in range(size)])


def sibling(x):
    return lax.ppermute(x, "chan", [(i, i ^ 1) for i in range(lax.axis_size("chan"))])


def dot(a, b):
    return jnp.dot(a, b, preferred_element_type=F32)


def after(x, *others):
    return lax.optimization_barrier((x,) + others)[0]


def anywhere():
    return pl.BlockSpec(memory_space=pl.ANY)


def whole(shape):
    return pl.BlockSpec(shape, lambda *_: (0,) * len(shape))


def call(kernel, grid, prefetch, operands, in_specs, outs, out_specs, scratch, name, micros=1, vmem=16):
    return pl.pallas_call(
        kernel,
        grid_spec=pltpu.PrefetchScalarGridSpec(
            num_scalar_prefetch=1,
            grid=grid,
            in_specs=in_specs,
            out_specs=out_specs,
            scratch_shapes=scratch,
        ),
        out_shape=outs,
        compiler_params=pltpu.CompilerParams(vmem_limit_bytes=vmem * MIB),
        cost_estimate=pl.CostEstimate(
            flops=micros * 10**9, bytes_accessed=micros << 20, transcendentals=0
        ),
        name=name,
    )(prefetch, *operands)


def short_filter(taps, before, block):
    longer = jnp.concatenate([before, block], 0)
    rows = block.shape[0]
    result = jnp.zeros(block.shape, F32)
    for lag in range(KERNEL):
        result = result + taps[lag] * longer[8 - lag : 8 - lag + rows]
    return result.astype(BF16)


def ends(rows):
    return jnp.concatenate([rows[:8].astype(F32), rows[-8:].astype(F32)], 0).astype(BF16)


def first_rows(taps, before, here):
    return short_filter(taps, before[8:].astype(F32), here[:8].astype(F32))


def gated(gate_in, values):
    return (gate_in.astype(F32) * values.astype(F32)).astype(BF16)


def project(pairs, chip_ids, core, me, w_in, conv_taps, groups, total=None):
    count = len(pairs)
    parts = [p for pair in pairs for block in pair for p in block]
    rows = sum(p.shape[0] for p in pairs[0][0])
    width = parts[0].shape[1]
    streams, _, out_width = w_in.shape
    depth = 2 * width
    share = out_width // groups
    split = share % 128 == 0
    finish = total is not None

    def kernel(ids, w_ref, *refs):
        part_refs, refs = refs[: len(parts)], refs[len(parts) :]
        if finish:
            total_ref, taps_ref, gate_ref, ends_ref, refs = *refs[:4], refs[4:]
            in_refs, refs = refs[: len(outs) - 2], refs[len(outs) - 2 :]
            x, kept, sums, sums_ready = refs
        else:
            out_ref, x, w, w_ready = refs
        s = pl.program_id(0)

        def w_copy(t, j):
            first = pl.multiple_of(ids[j] * depth, depth)
            return pltpu.make_async_copy(
                w_ref.at[t, pl.ds(first, depth)],
                w.at[t, pl.ds(j * depth, depth)],
                w_ready.at[t, j],
            )

        def sum_copy(t):
            return pltpu.make_async_copy(total_ref.at[t], sums.at[t], sums_ready.at[t])

        @pl.when(s == 0)
        def _():
            for t in range(streams):
                if finish:
                    sum_copy(t).start()
                else:
                    for j in range(count):
                        w_copy(t, j).start()
            at = 0
            for j in range(count):
                for block, side in ((pairs[j][0], ids[count]), (pairs[j][1], 1 - ids[count])):
                    place = pl.ds(pl.multiple_of(j * depth + side * width, width), width)
                    row = 0
                    for ref in part_refs[at : at + len(block)]:
                        x[row : row + ref.shape[0], place] = ref[...]
                        row += ref.shape[0]
                    at += len(block)

        if not finish:
            for j in range(count):
                w_copy(s, j).wait()
            out_ref[0] = dot(x[...], w[s])
            return
        new = dot(x[...], w_ref[0])
        sum_copy(s).wait()
        rounded = (new + sums[s]).astype(BF16)
        filtered = short_filter(taps_ref, jnp.zeros((8, out_width), F32), rounded.astype(F32))
        kept[s, :rows] = filtered
        kept[s, rows:] = ends(rounded)

        @pl.when(s == streams - 1)
        def _():
            gate_ref[...] = kept[0, :rows]
            ends_ref[...] = kept[0, rows:]
            kept[0, :rows] = gated(kept[1, :rows], kept[2, :rows])
            for slot in range(groups if split else 1):
                q = pl.multiple_of(partner(ids[count + 1], slot, groups) * share, share)
                columns = pl.ds(q, share) if split else slice(None)
                in_refs[slot][:rows] = kept[0, :rows, columns]
                for t in range(1, streams):
                    place = rows + (t - 1) * EDGE
                    in_refs[slot][place : place + EDGE] = kept[t, rows:, columns]

    in_specs = [whole(p.shape) for p in parts]
    operands = [w_in] + parts
    scratch = [pltpu.VMEM((rows, count * depth), BF16)]

    def by_stream(extent):
        return pl.BlockSpec((1, extent, out_width), lambda s, ids: (s, 0, 0))

    if finish:
        taps_spec = pl.BlockSpec((KERNEL, pl.squeezed, 1, out_width), lambda s, ids: (0, s, 0, 0))
        in_specs = [by_stream(depth)] + in_specs + [anywhere(), taps_spec]
        operands += [total, conv_taps]
        longer = rows + (streams - 1) * EDGE
        outs = [pltpu.HBM((rows, out_width), BF16), pltpu.HBM((EDGE, out_width), BF16)]
        outs += [pltpu.HBM((longer, share if split else out_width), BF16)] * (groups if split else 1)
        out_specs = [whole(o.shape) for o in outs]
        scratch += [
            pltpu.VMEM((streams, rows + EDGE, out_width), BF16),
            pltpu.VMEM((streams, rows, out_width), F32),
            pltpu.SemaphoreType.DMA((streams,)),
        ]
    else:
        in_specs = [anywhere()] + in_specs
        outs = [pltpu.HBM((streams, rows, out_width), F32)]
        out_specs = [by_stream(rows)]
        scratch += [
            pltpu.VMEM((streams, count * depth, out_width), BF16),
            pltpu.SemaphoreType.DMA((streams, count)),
        ]
    found = call(
        kernel,
        (streams,),
        jnp.stack(list(chip_ids) + [core, me]).astype(jnp.int32),
        operands,
        in_specs,
        outs,
        out_specs,
        scratch,
        "project",
        4 if finish else 20,
        16 if finish else 51,
    )
    if not finish:
        return found[0]
    gate, gate_ends, ins = found[0], found[1], list(found[2:])
    return gate, gate_ends, (ins if split else by_slot(ins[0], groups, me))


def by_slot(block, groups, me):
    stack = jnp.stack(jnp.split(block, groups, axis=1))
    return [
        lax.dynamic_index_in_dim(stack, partner(me, slot, groups), 0, keepdims=False)
        for slot in range(groups)
    ]


def partner(me, slot, groups):
    if groups & (groups - 1) == 0:
        return me ^ slot
    return (me + slot) % groups


def source(me, slot, groups):
    if groups & (groups - 1) == 0:
        return me ^ slot
    return (me - slot + groups) % groups


def taps_spectra(pieces, forward, back, me):
    groups = len(pieces)
    span, share = pieces[0].shape

    def kernel(at, *refs):
        piece_refs, refs = refs[:groups], refs[groups:]
        forward_ref, back_ref, out_ref, forward_out, back_out, padded = refs
        row_ids = lax.broadcasted_iota(jnp.int32, (span, share), 0)
        for s in range(groups):
            k = source(at[0], s, groups)
            block = piece_refs[s][...]
            padded[0:span, pl.ds(pl.multiple_of(k * share, share), share)] = block

            @pl.when(k < groups - 1)
            def _():
                place = pl.multiple_of((k + 1) * share, share)
                kept = jnp.where(row_ids == 0, 0.0, block.astype(F32)).astype(BF16)
                padded[span : 2 * span, pl.ds(place, share)] = kept

        padded[span : 2 * span, 0:share] = jnp.zeros((span, share), BF16)
        out_ref[...] = dot(forward_ref[...], padded[...]).astype(BF16)
        forward_out[...] = forward_ref[:, 0:span]
        back_out[...] = back_ref[...]

    shape = (2 * span, groups * share)
    outs = [
        jax.ShapeDtypeStruct(shape, BF16),
        jax.ShapeDtypeStruct((2 * span, span), BF16),
        jax.ShapeDtypeStruct(back.shape, BF16),
    ]
    operands = list(pieces) + [forward, back]
    return call(
        kernel,
        (1,),
        me[None],
        operands,
        [whole(o.shape) for o in operands],
        outs,
        [whole(o.shape) for o in outs],
        [pltpu.VMEM(shape, BF16)],
        "taps_spectra",
        2,
    )


def long_filter(pieces, taps, spectra_taps, forward_in, back, skip, me):
    groups = len(pieces)
    share = pieces[0].shape[1]
    span = back.shape[0]
    cols = groups * share
    step = 16

    def kernel(at, *refs):
        ins, refs = refs[:groups], refs[groups:]
        short_ref, taps_ref, forward_ref, back_ref, skip_ref = refs[:5]
        outs, (signal, spectra, mixture, result, tails) = refs[5 : 5 + groups], refs[5 + groups :]
        for s in range(groups):
            j = source(at[0], s, groups)
            signal[:, pl.ds(pl.multiple_of(j * share, share), share)] = ins[s][0:span]
            tails[j] = ins[s][span:]
        for j in range(groups):
            heads = []
            for t in (0, 1):
                here = tails[j, t * EDGE : (t + 1) * EDGE]
                before = tails[j - 1, t * EDGE : (t + 1) * EDGE] if j else jnp.zeros_like(here)
                heads.append(first_rows([short_ref[lag, t + 1] for lag in range(KERNEL)], before, here))
            place = slice(j * share, (j + 1) * share)
            rest = signal[0:EDGE, place].astype(F32)[8:]
            head = jnp.concatenate([gated(*heads).astype(F32), rest], 0)
            signal[0:EDGE, place] = head.astype(BF16)
        spectra[...] = dot(forward_ref[...], signal[...]).astype(BF16)

        def mix(start, special):
            def read(ref, first, block):
                return ref[pl.ds(first, step), block * share : (block + 1) * share].astype(F32)

            imag_start = start + span
            real_g = [read(taps_ref, start, b) for b in range(groups)]
            imag_g = [read(taps_ref, imag_start, b) for b in range(groups)]
            real_u = [read(spectra, start, b) for b in range(groups)]
            imag_u = [read(spectra, imag_start, b) for b in range(groups)]
            first = lax.broadcasted_iota(jnp.int32, (step, share), 0) == 0
            for i in range(groups):
                real = imag = None
                for j in range(i + 1):
                    rr = real_g[i - j] * real_u[j]
                    ii = imag_g[i - j] * imag_u[j]
                    cross = real_g[i - j] * imag_u[j] + imag_g[i - j] * real_u[j]
                    new_real, new_imag = rr - ii, cross
                    if special:
                        new_real = jnp.where(first, rr, new_real)
                        new_imag = jnp.where(first, ii, new_imag)
                    real = new_real if real is None else real + new_real
                    imag = new_imag if imag is None else imag + new_imag
                place = slice(i * share, (i + 1) * share)
                mixture[pl.ds(start, step), place] = real.astype(BF16)
                mixture[pl.ds(imag_start, step), place] = imag.astype(BF16)

        mix(0, True)

        @pl.loop(1, span // step)
        def _(c):
            mix(pl.multiple_of(c * step, step), False)

        result[...] = (
            dot(back_ref[...], mixture[...]) + skip_ref[...] * signal[...].astype(F32)
        ).astype(BF16)
        for s in range(groups):
            j = pl.multiple_of(partner(at[0], s, groups) * share, share)
            outs[s][...] = result[:, pl.ds(j, share)]

    operands = list(pieces) + [taps, spectra_taps, forward_in, back, skip]
    in_specs = [whole(o.shape) for o in operands]
    outs = [jax.ShapeDtypeStruct((span, share), BF16)] * groups
    return call(
        kernel,
        (1,),
        me[None],
        operands,
        in_specs,
        outs,
        [whole(o.shape) for o in outs],
        [
            pltpu.VMEM((span, cols), BF16),
            pltpu.VMEM((2 * span, cols), BF16),
            pltpu.VMEM((2 * span, cols), BF16),
            pltpu.VMEM((span, cols), BF16),
            pltpu.VMEM((groups, 2 * EDGE, share), BF16),
        ],
        "long_filter",
        3,
    )


def gate_blocks(gate, before, here, taps, pieces, me):
    groups = len(pieces)
    rows, share = pieces[0].shape

    def kernel(at, gate_ref, before_ref, here_ref, taps_ref, *refs):
        out = refs[groups]
        head = first_rows([taps_ref[lag, 0] for lag in range(KERNEL)], before_ref[...], here_ref[...])
        rest = gate_ref[0:EDGE].astype(F32)[8:]
        edge_ref = refs[groups + 1]
        edge_ref[...] = jnp.concatenate([head.astype(F32), rest], 0).astype(BF16)
        for s in range(groups):
            place = pl.ds(pl.multiple_of(source(at[0], s, groups) * share, share), share)
            out[:, place] = gated(gate_ref[:, place], refs[s][...])
            out[0:EDGE, place] = gated(edge_ref[:, place], refs[s][0:EDGE])

    operands = [gate, before, here, taps] + list(pieces)
    return call(
        kernel,
        (1,),
        me[None],
        operands,
        [whole(o.shape) for o in operands],
        jax.ShapeDtypeStruct(gate.shape, BF16),
        whole(gate.shape),
        [pltpu.VMEM(here.shape, BF16)],
        "gate_blocks",
    )


def output_shares(gated, other, w_own, w_other, chip_ids, plan):
    count = len(chip_ids)
    rows, width = gated.shape
    cols = w_other.shape[1] * 2 // lax.axis_size("chan")

    def kernel(_, a_ref, b_ref, w_ref, v_ref, *outs):
        k = pl.program_id(0)
        total = dot(a_ref[...], w_ref[...]) + dot(b_ref[...], v_ref[...])
        at = 0
        for j in range(count):
            here = outs[at : at + len(plan[j])]
            at += len(plan[j])

            @pl.when(k == j)
            def _():
                for out, (first, last, kind) in zip(here, plan[j]):
                    out[...] = total[first:last].astype(kind)

    outs = [
        jax.ShapeDtypeStruct((last - first, cols), kind)
        for parts in plan
        for first, last, kind in parts
    ]
    return call(
        kernel,
        (count,),
        jnp.stack(list(chip_ids)).astype(jnp.int32),
        [gated, other, w_own, w_other],
        [
            whole(gated.shape),
            whole(other.shape),
            pl.BlockSpec((width, cols), lambda k, ids: (0, ids[k])),
            pl.BlockSpec((width, cols), lambda k, ids: (0, ids[k])),
        ],
        outs,
        [whole(o.shape) for o in outs],
        [],
        "output_shares",
    )


def add_up(own, extras):
    span, cols = own.shape
    half = span // 2
    flat = [e for side in extras for e in side]

    def kernel(_, own_ref, *refs):
        at = 0
        for k, side in enumerate(extras):
            total = own_ref[k * half : (k + 1) * half]
            for ref in refs[at : at + len(side)]:
                total = total + ref[...].astype(F32)
            at += len(side)
            refs[-1][k * half : (k + 1) * half] = total.astype(BF16)

    return call(
        kernel,
        (1,),
        jnp.zeros((1,), jnp.int32),
        [own] + flat,
        [whole(own.shape)] + [whole(e.shape) for e in flat],
        jax.ShapeDtypeStruct(own.shape, BF16),
        whole(own.shape),
        [],
        "add_up",
    )


def exchange(piece):
    groups = lax.axis_size("ctx")

    def send(slot):
        route = [(i, partner(i, slot, groups)) for i in range(groups)]
        return lax.ppermute(piece(slot), "ctx", route)

    return [piece(0)] + [send(s) for s in range(1, groups)]


def in_order(blocks, me):
    groups = len(blocks)
    result = jnp.zeros((groups,) + blocks[0].shape, blocks[0].dtype)
    for s, b in enumerate(blocks):
        result = lax.dynamic_update_index_in_dim(result, b, source(me, s, groups), 0)
    return jnp.concatenate(list(result), 1)


def taps_spectra_plain(pieces, forward, back, me):
    groups = len(pieces)
    span, share = pieces[0].shape
    taps = in_order(pieces, me)
    before = jnp.concatenate(
        [jnp.zeros((span, share), BF16), taps[:, : (groups - 1) * share]], 1
    )
    before = jnp.where(lax.broadcasted_iota(jnp.int32, (span, 1), 0) == 0, 0, before)
    spectra = dot(forward, jnp.concatenate([taps, before], 0)).astype(BF16)
    return spectra, forward[:, :span], back


def long_filter_plain(pieces, taps, spectra_taps, forward_in, back, skip, me):
    groups = len(pieces)
    span, share = back.shape[0], pieces[0].shape[1]
    pieces = in_order(pieces, me)
    tails = [pieces[span + t * EDGE : span + (t + 1) * EDGE] for t in (0, 1)]
    heads = []
    for t in (0, 1):
        before = jnp.concatenate([jnp.zeros((EDGE, share), BF16), tails[t][:, :-share]], 1)
        wide = [jnp.tile(taps[lag, t + 1], (1, groups)) for lag in range(KERNEL)]
        heads.append(first_rows(wide, before, tails[t]))
    signal = jnp.concatenate([gated(*heads), pieces[8:span]], 0)
    spectra = dot(forward_in, signal).astype(BF16)
    real_g, imag_g = spectra_taps[:span].astype(F32), spectra_taps[span:].astype(F32)
    real_u, imag_u = spectra[:span].astype(F32), spectra[span:].astype(F32)
    first = lax.broadcasted_iota(jnp.int32, (span, 1), 0) == 0
    mixed = []
    for i in range(groups):
        real = imag = 0.0
        for j in range(i + 1):
            g = slice((i - j) * share, (i - j + 1) * share)
            u = slice(j * share, (j + 1) * share)
            rr = real_g[:, g] * real_u[:, u]
            ii = imag_g[:, g] * imag_u[:, u]
            cross = real_g[:, g] * imag_u[:, u] + imag_g[:, g] * real_u[:, u]
            real = real + jnp.where(first, rr, rr - ii)
            imag = imag + jnp.where(first, ii, cross)
        mixed.append(jnp.concatenate([real, imag], 0).astype(BF16))
    result = dot(back, jnp.concatenate(mixed, 1)) + skip * signal.astype(F32)
    result = jnp.stack(jnp.split(result.astype(BF16), groups, axis=1))
    found = []
    for s in range(groups):
        block = lax.dynamic_index_in_dim(result, partner(me, s, groups), 0, keepdims=False)
        found.append(block)
    return found


def gate_blocks_plain(gate, before, here, taps, pieces, me):
    head = first_rows([taps[lag, 0] for lag in range(KERNEL)], before, here)
    return gated(jnp.concatenate([head, gate[8:]], 0), in_order(pieces, me))


def body(inputs, w_in, conv_taps, skip_gain, filter_taps, w_out):
    span, width = inputs.shape
    half = span // 2
    groups = lax.axis_size("ctx")
    me = lax.axis_index("ctx")
    chips = lax.axis_size("chan") // 2
    reach = chips // 2
    place = lax.axis_index("chan")
    chip, core = place // 2, place % 2
    share = width // groups
    aligned = share % 128 == 0
    out_width = w_out.shape[1] // (2 * chips)
    forward_np, back_np = half_tables(span)
    forward, back = jnp.asarray(forward_np), jnp.asarray(back_np)
    w_streams = jnp.transpose(w_in, (1, 0, 2))
    short_taps = conv_taps.astype(F32)[:, :, None]

    split_taps = [filter_taps[:, q * share : (q + 1) * share] for q in range(groups)]
    split_taps = jnp.stack(split_taps)

    def pick(stack):
        return lambda s: lax.dynamic_index_in_dim(
            stack, partner(me, s, groups), 0, keepdims=False
        )

    tap_blocks = exchange(pick(split_taps))

    def columns(w, parity):
        starts = [(2 * z + parity) * out_width for z in range(chips)]
        return jnp.concatenate([lax.dynamic_slice_in_dim(w, c, out_width, 1) for c in starts], 1)

    w_given = columns(w_out, 1 - core)
    w_far = lax.dynamic_slice_in_dim(w_streams, (chip + reach) % chips * 2 * width, 2 * width, 1)

    skip = lax.dynamic_slice_in_dim(skip_gain, me * share, share, 0)
    skip = jnp.tile(skip, groups)[None]
    share_taps = lax.dynamic_slice_in_dim(short_taps, me * share, share, 3)

    found = [(0, [inputs])]
    up = [inputs[:half], inputs[half:]]
    down = list(up)
    for d in range(1, reach):
        up_top, down_low = shift(up[0], "chan", 2), shift(down[1], "chan", -2)
        up_low, down_top = shift(up[1], "chan", 2), shift(down[0], "chan", -2)
        if d == reach - 1:
            up_top, down_low, tap_blocks, w_given, w_far, skip, share_taps = lax.optimization_barrier(
                (up_top, down_low, tap_blocks, w_given, w_far, skip, share_taps)
            )
        up, down = [up_top, up_low], [down_top, down_low]
        found += [(d, up), (-d, down)]
    far = [shift(up[0], "chan", 2), shift(down[1], "chan", -2)]

    def both(blocks):
        return blocks, [sibling(b) for b in blocks]

    def added(blocks, w, total=None):
        return project(
            [both(b) for _, b in blocks],
            [(chip - d) % chips for d, _ in blocks],
            core,
            me,
            w,
            short_taps,
            groups,
            total,
        )

    total = added(found, w_streams)
    far = [after(f, total) for f in far]
    gate, gate_ends, pieces = added([(reach, far)], w_far, total)

    pieces_in = exchange(lambda s: pieces[s])
    before = shift(gate_ends, "ctx", 1)
    before = jnp.where(me > 0, before, jnp.zeros_like(before))

    tap_blocks = [after(t, before) for t in tap_blocks]
    spectra_taps, forward_in, back = (taps_spectra if aligned else taps_spectra_plain)(
        tap_blocks, forward, back, me
    )
    w_own = columns(after(w_out, spectra_taps), core)

    w_other = sibling(after(w_given, gate))

    filtered = (long_filter if aligned else long_filter_plain)(
        pieces_in, share_taps, spectra_taps, forward_in, back, after(skip, w_own), me
    )
    filtered = lax.optimization_barrier((list(filtered), w_other))[0]
    gated_out = (gate_blocks if aligned else gate_blocks_plain)(
        gate, before, gate_ends, short_taps, exchange(lambda s: filtered[s]), me
    )

    other = sibling(gated_out)

    def shares(offsets, plan):
        ids = [(chip + d) % chips for d in offsets]
        return output_shares(gated_out, other, w_own, w_other, ids, plan)

    up_top, down_low = shares([reach], [[(0, half, BF16), (half, span, BF16)]])
    offsets, plan = [], []
    for d in range(reach - 1, 0, -1):
        last = d == reach - 1
        offsets += [d, -d]
        plan.append([(0, half, F32), (half, span, BF16 if last else F32)])
        plan.append([(0, half, BF16 if last else F32), (half, span, F32)])
    kept = list(shares(offsets + [0], plan + [[(0, span, F32)]]))
    up_top, down_low = shift(up_top, "chan", 2), shift(down_low, "chan", -2)
    up_low = down_top = None

    def step(carried, new, distance):
        if carried is not None:
            new = (carried.astype(F32) + new).astype(BF16)
        return shift(new, "chan", distance)

    for k in range(reach - 1):
        ahead_top, ahead_low, behind_top, behind_low = kept[4 * k : 4 * k + 4]
        up_low, down_top = step(up_low, ahead_low, 2), step(down_top, behind_top, -2)
        up_top, down_low = step(up_top, ahead_top, 2), step(down_low, behind_low, -2)
    extras = [[up_top], [down_low]]
    if reach > 1:
        extras = [[up_top, down_top], [up_low, down_low]]
    return add_up(kept[-1], extras)


def solution(mesh):
    return jax.shard_map(
        body,
        mesh=mesh,
        in_specs=(
            P("ctx", "chan"),
            P(None, None, "chan"),
            P(None, None, "chan"),
            P("chan"),
            P("ctx", "chan"),
            P("chan", None),
        ),
        out_specs=P("ctx", "chan"),
        check_vma=False,
    )
```

```python
import math

import jax
import jax.numpy as jnp
import ml_dtypes
import numpy as np
from jax import lax
from jax.experimental import pallas as pl
from jax.experimental.pallas import tpu as pltpu
from jax.sharding import PartitionSpec as P

KERNEL = 3
EDGE = 16
BF16 = jnp.bfloat16
F32 = jnp.float32
MIB = 1 << 20


def half_tables(span):
    n = 2 * span
    f = np.arange(span)[:, None]
    m = np.arange(n)[None, :]
    ang = 2.0 * math.pi * ((f * m) % n) / n
    real = np.cos(ang)
    imag = -np.sin(ang)
    imag[0] = np.where(np.arange(n) % 2 == 0, 1.0, -1.0)
    forward = np.concatenate([real, imag], 0).astype(ml_dtypes.bfloat16)
    weight = np.full((n, 1), 2.0 / n)
    weight[0] = 1.0 / n
    weight[span] = 1.0 / n
    back = (np.concatenate([real, imag], 0) * weight)[:, :span].T
    return forward, np.ascontiguousarray(back).astype(ml_dtypes.bfloat16)


def shift(x, axis, distance):
    size = lax.axis_size(axis)
    return lax.ppermute(x, axis, [(i, (i + distance) % size) for i in range(size)])


def sibling(x):
    return lax.ppermute(x, "chan", [(i, i ^ 1) for i in range(lax.axis_size("chan"))])


def dot(a, b):
    return jnp.dot(a, b, preferred_element_type=F32)


def after(x, *others):
    return lax.optimization_barrier((x,) + others)[0]


def anywhere():
    return pl.BlockSpec(memory_space=pl.ANY)


def whole(shape):
    return pl.BlockSpec(shape, lambda *_: (0,) * len(shape))


def call(kernel, grid, prefetch, operands, in_specs, outs, out_specs, scratch, name, micros=1, vmem=16):
    return pl.pallas_call(
        kernel,
        grid_spec=pltpu.PrefetchScalarGridSpec(
            num_scalar_prefetch=1,
            grid=grid,
            in_specs=in_specs,
            out_specs=out_specs,
            scratch_shapes=scratch,
        ),
        out_shape=outs,
        compiler_params=pltpu.CompilerParams(vmem_limit_bytes=vmem * MIB),
        cost_estimate=pl.CostEstimate(
            flops=micros * 10**9, bytes_accessed=micros << 20, transcendentals=0
        ),
        name=name,
    )(prefetch, *operands)


def short_filter(taps, before, block):
    longer = jnp.concatenate([before, block], 0)
    rows = block.shape[0]
    result = jnp.zeros(block.shape, F32)
    for lag in range(KERNEL):
        result = result + taps[lag] * longer[8 - lag : 8 - lag + rows]
    return result.astype(BF16)


def first_rows(taps, before, here):
    return short_filter(taps, before[8:].astype(F32), here[:8].astype(F32))


def gated(gate_in, values):
    return (gate_in.astype(F32) * values.astype(F32)).astype(BF16)


def start_copies(copies):
    for copy in copies:
        copy.start()


def wait_copies(copies):
    for copy in copies:
        copy.wait()


def project_most(pairs, chip_ids, core, w_in):
    count = len(pairs)
    parts = [p for pair in pairs for block in pair for p in block]
    rows = sum(p.shape[0] for p in pairs[0][0])
    half = rows // 2
    width = parts[0].shape[1]
    streams, _, out_width = w_in.shape
    depth = 2 * width
    most = (count - 1) * depth

    def kernel(ids, w_ref, *refs):
        part_refs, refs = refs[: len(parts)], refs[len(parts) :]
        top_ref, low_ref, x, far, w, x_ready, w_ready = refs
        s = pl.program_id(0)

        def w_copies(t):
            for j in range(count):
                first = pl.multiple_of(ids[j] * depth, depth)
                yield pltpu.make_async_copy(
                    w_ref.at[t, pl.ds(first, depth)],
                    w.at[t, j * depth : (j + 1) * depth],
                    w_ready.at[t, j],
                )

        def x_copies():
            at = 0
            for j in range(count):
                for block, side in ((pairs[j][0], ids[count]), (pairs[j][1], 1 - ids[count])):
                    row = 0
                    base = j * depth if j < count - 1 else 0
                    place = pl.ds(pl.multiple_of(base + side * width, width), width)
                    for part in block:
                        target = (x if j < count - 1 else far).at[row : row + part.shape[0], place]
                        yield pltpu.make_async_copy(part_refs[at], target, x_ready.at[at])
                        row += part.shape[0]
                        at += 1

        @pl.when(s == 0)
        def _():
            start_copies(w_copies(0))
            start_copies(x_copies())
            for t in range(1, streams):
                start_copies(w_copies(t))
            wait_copies(x_copies())

        wait_copies(w_copies(s))
        total = dot(x[...], w[s, :most])
        top_ref[0] = (total[:half] + dot(far[...], w[s, most:])).astype(BF16)
        low_ref[0] = total[half:]

    def by_stream():
        return pl.BlockSpec((1, half, out_width), lambda s, ids: (s, 0, 0))

    shape = (streams, half, out_width)
    return call(
        kernel,
        (streams,),
        jnp.stack(list(chip_ids) + [core]).astype(jnp.int32),
        [w_in] + parts,
        [anywhere()] * (1 + len(parts)),
        [jax.ShapeDtypeStruct(shape, BF16), jax.ShapeDtypeStruct(shape, F32)],
        [by_stream(), by_stream()],
        [
            pltpu.VMEM((rows, most), BF16),
            pltpu.VMEM((half, depth), BF16),
            pltpu.VMEM((streams, most + depth, out_width), BF16),
            pltpu.SemaphoreType.DMA((len(parts),)),
            pltpu.SemaphoreType.DMA((streams, count)),
        ],
        "project_most",
        8,
        24,
    )


def project_rest(pair, core, me, w_far, top, low, conv_taps, groups):
    streams, half, out_width = top.shape
    rows = 2 * half
    width = pair[0].shape[1]
    depth = 2 * width
    share = out_width // groups
    split = share % 128 == 0
    order = list(range(1, streams)) + [0]

    def kernel(at, own_ref, other_ref, w_ref, top_ref, low_ref, taps_ref, gate_ref, ends_ref, *refs):
        in_refs, refs = refs[: len(ins)], refs[len(ins) :]
        x, w, tops, lows, kept, x_ready, ready = refs

        def x_copies():
            for k, (ref, side) in enumerate(((own_ref, at[0]), (other_ref, 1 - at[0]))):
                place = pl.ds(pl.multiple_of(side * width, width), width)
                yield pltpu.make_async_copy(ref, x.at[:, place], x_ready.at[k])

        def copies(t):
            for k, (ref, target) in enumerate(((w_ref, w), (low_ref, lows), (top_ref, tops))):
                yield pltpu.make_async_copy(ref.at[t], target.at[t], ready.at[t, k])

        start_copies(x_copies())
        for t in order:
            start_copies(copies(t))
        wait_copies(x_copies())
        for t in order:
            wait_copies(copies(t))
            bottom = (dot(x[...], w[t]) + lows[t]).astype(BF16)
            upper = tops[t]
            taps = [taps_ref[lag, t] for lag in range(KERNEL)]
            first = upper.astype(F32)
            kept[t, :half] = short_filter(taps, jnp.zeros((8, out_width), F32), first)
            kept[t, half:rows] = short_filter(taps, first[half - 8 :], bottom.astype(F32))
            ends = jnp.concatenate([first[:8], bottom.astype(F32)[half - 8 :]], 0)
            kept[t, rows:] = ends.astype(BF16)
        gate_ref[...] = kept[0, :rows]
        ends_ref[...] = kept[0, rows:]
        kept[0, :rows] = gated(kept[1, :rows], kept[2, :rows])
        for slot in range(len(ins)):
            q = pl.multiple_of(partner(at[1], slot, groups) * share, share)
            columns = pl.ds(q, share) if split else slice(None)
            in_refs[slot][:rows] = kept[0, :rows, columns]
            for t in range(1, streams):
                place = rows + (t - 1) * EDGE
                in_refs[slot][place : place + EDGE] = kept[t, rows:, columns]

    longer = rows + (streams - 1) * EDGE
    ins = [pltpu.HBM((longer, share if split else out_width), BF16)] * (groups if split else 1)
    outs = [pltpu.HBM((rows, out_width), BF16), pltpu.HBM((EDGE, out_width), BF16)] + ins
    found = call(
        kernel,
        (1,),
        jnp.stack([core, me]).astype(jnp.int32),
        list(pair) + [w_far, top, low, conv_taps],
        [anywhere()] * 5 + [whole(conv_taps.shape)],
        outs,
        [whole(o.shape) for o in outs],
        [
            pltpu.VMEM((half, depth), BF16),
            pltpu.VMEM(w_far.shape, BF16),
            pltpu.VMEM(top.shape, BF16),
            pltpu.VMEM(low.shape, F32),
            pltpu.VMEM((streams, rows + EDGE, out_width), BF16),
            pltpu.SemaphoreType.DMA((2,)),
            pltpu.SemaphoreType.DMA((streams, 3)),
        ],
        "project_rest",
        1,
        24,
    )
    gate, ends, ins = found[0], found[1], list(found[2:])
    return gate, ends, (ins if split else by_slot(ins[0], groups, me))


def by_slot(block, groups, me):
    stack = jnp.stack(jnp.split(block, groups, axis=1))
    return [
        lax.dynamic_index_in_dim(stack, partner(me, slot, groups), 0, keepdims=False)
        for slot in range(groups)
    ]


def partner(me, slot, groups):
    if groups & (groups - 1) == 0:
        return me ^ slot
    return (me + slot) % groups


def source(me, slot, groups):
    if groups & (groups - 1) == 0:
        return me ^ slot
    return (me - slot + groups) % groups


def taps_spectra(pieces, forward, back, me):
    groups = len(pieces)
    span, share = pieces[0].shape

    def kernel(at, *refs):
        piece_refs, refs = refs[:groups], refs[groups:]
        forward_ref, out_ref, padded = refs
        row_ids = lax.broadcasted_iota(jnp.int32, (span, share), 0)
        for s in range(groups):
            k = source(at[0], s, groups)
            block = piece_refs[s][...]
            padded[0:span, pl.ds(pl.multiple_of(k * share, share), share)] = block

            @pl.when(k < groups - 1)
            def _():
                place = pl.multiple_of((k + 1) * share, share)
                kept = jnp.where(row_ids == 0, 0.0, block.astype(F32)).astype(BF16)
                padded[span : 2 * span, pl.ds(place, share)] = kept

        padded[span : 2 * span, 0:share] = jnp.zeros((span, share), BF16)
        out_ref[...] = dot(forward_ref[...], padded[...]).astype(BF16)

    shape = (2 * span, groups * share)
    outs = [pltpu.HBM(shape, BF16)]
    operands = list(pieces) + [forward]
    (spectra,) = call(
        kernel,
        (1,),
        me[None],
        operands,
        [whole(o.shape) for o in operands],
        outs,
        [whole(o.shape) for o in outs],
        [pltpu.VMEM(shape, BF16)],
        "taps_spectra",
        20,
    )
    return spectra, None, back


def long_filter(pieces, taps, spectra_taps, forward_in, back, skip, me):
    groups = len(pieces)
    share = pieces[0].shape[1]
    span = back.shape[0]
    cols = groups * share
    step = 16

    def kernel(at, *refs):
        ins, refs = refs[:groups], refs[groups:]
        short_ref, taps_ref, forward_ref, back_ref, skip_ref = refs[:5]
        outs, (signal, spectra, mixture, result, tails) = refs[5 : 5 + groups], refs[5 + groups :]
        for s in range(groups):
            j = source(at[0], s, groups)
            signal[:, pl.ds(pl.multiple_of(j * share, share), share)] = ins[s][0:span]
            tails[j] = ins[s][span:]
        for j in range(groups):
            heads = []
            for t in (0, 1):
                here = tails[j, t * EDGE : (t + 1) * EDGE]
                before = tails[j - 1, t * EDGE : (t + 1) * EDGE] if j else jnp.zeros_like(here)
                heads.append(first_rows([short_ref[lag, t + 1] for lag in range(KERNEL)], before, here))
            place = slice(j * share, (j + 1) * share)
            rest = signal[0:EDGE, place].astype(F32)[8:]
            head = jnp.concatenate([gated(*heads).astype(F32), rest], 0)
            signal[0:EDGE, place] = head.astype(BF16)
        spectra[...] = dot(forward_ref[...], signal[...]).astype(BF16)

        def mix(start, special):
            def read(ref, first, block):
                return ref[pl.ds(first, step), block * share : (block + 1) * share].astype(F32)

            imag_start = start + span
            real_g = [read(taps_ref, start, b) for b in range(groups)]
            imag_g = [read(taps_ref, imag_start, b) for b in range(groups)]
            real_u = [read(spectra, start, b) for b in range(groups)]
            imag_u = [read(spectra, imag_start, b) for b in range(groups)]
            first = lax.broadcasted_iota(jnp.int32, (step, share), 0) == 0
            for i in range(groups):
                real = imag = None
                for j in range(i + 1):
                    rr = real_g[i - j] * real_u[j]
                    ii = imag_g[i - j] * imag_u[j]
                    cross = real_g[i - j] * imag_u[j] + imag_g[i - j] * real_u[j]
                    new_real, new_imag = rr - ii, cross
                    if special:
                        new_real = jnp.where(first, rr, new_real)
                        new_imag = jnp.where(first, ii, new_imag)
                    real = new_real if real is None else real + new_real
                    imag = new_imag if imag is None else imag + new_imag
                place = slice(i * share, (i + 1) * share)
                mixture[pl.ds(start, step), place] = real.astype(BF16)
                mixture[pl.ds(imag_start, step), place] = imag.astype(BF16)

        mix(0, True)

        @pl.loop(1, span // step)
        def _(c):
            mix(pl.multiple_of(c * step, step), False)

        result[...] = (
            dot(back_ref[...], mixture[...]) + skip_ref[...] * signal[...].astype(F32)
        ).astype(BF16)
        for s in range(groups):
            j = pl.multiple_of(partner(at[0], s, groups) * share, share)
            outs[s][...] = result[:, pl.ds(j, share)]

    operands = list(pieces) + [taps, spectra_taps, forward_in, back, skip]
    in_specs = [whole(o.shape) for o in operands]
    outs = [jax.ShapeDtypeStruct((span, share), BF16)] * groups
    return call(
        kernel,
        (1,),
        me[None],
        operands,
        in_specs,
        outs,
        [whole(o.shape) for o in outs],
        [
            pltpu.VMEM((span, cols), BF16),
            pltpu.VMEM((2 * span, cols), BF16),
            pltpu.VMEM((2 * span, cols), BF16),
            pltpu.VMEM((span, cols), BF16),
            pltpu.VMEM((groups, 2 * EDGE, share), BF16),
        ],
        "long_filter",
        3,
    )


def gate_blocks(gate, before, here, taps, pieces, me):
    groups = len(pieces)
    rows, share = pieces[0].shape

    def kernel(at, gate_ref, before_ref, here_ref, taps_ref, *refs):
        out = refs[groups]
        head = first_rows([taps_ref[lag, 0] for lag in range(KERNEL)], before_ref[...], here_ref[...])
        rest = gate_ref[0:EDGE].astype(F32)[8:]
        edge_ref = refs[groups + 1]
        edge_ref[...] = jnp.concatenate([head.astype(F32), rest], 0).astype(BF16)
        for s in range(groups):
            place = pl.ds(pl.multiple_of(source(at[0], s, groups) * share, share), share)
            out[:, place] = gated(gate_ref[:, place], refs[s][...])
            out[0:EDGE, place] = gated(edge_ref[:, place], refs[s][0:EDGE])

    operands = [gate, before, here, taps] + list(pieces)
    return call(
        kernel,
        (1,),
        me[None],
        operands,
        [whole(o.shape) for o in operands],
        jax.ShapeDtypeStruct(gate.shape, BF16),
        whole(gate.shape),
        [pltpu.VMEM(here.shape, BF16)],
        "gate_blocks",
    )


def output_shares(gated, other, w_own, w_other, chip_ids, plan):
    count = len(chip_ids)
    rows, width = gated.shape
    cols = w_other.shape[1] * 2 // lax.axis_size("chan")

    def kernel(_, a_ref, b_ref, w_ref, v_ref, *outs):
        k = pl.program_id(0)
        total = dot(a_ref[...], w_ref[...]) + dot(b_ref[...], v_ref[...])
        at = 0
        for j in range(count):
            here = outs[at : at + len(plan[j])]
            at += len(plan[j])

            @pl.when(k == j)
            def _():
                for out, (first, last, kind) in zip(here, plan[j]):
                    out[...] = total[first:last].astype(kind)

    outs = [
        jax.ShapeDtypeStruct((last - first, cols), kind)
        for parts in plan
        for first, last, kind in parts
    ]
    return call(
        kernel,
        (count,),
        jnp.stack(list(chip_ids)).astype(jnp.int32),
        [gated, other, w_own, w_other],
        [
            whole(gated.shape),
            whole(other.shape),
            pl.BlockSpec((width, cols), lambda k, ids: (0, ids[k])),
            pl.BlockSpec((width, cols), lambda k, ids: (0, ids[k])),
        ],
        outs,
        [whole(o.shape) for o in outs],
        [],
        "output_shares",
    )


def add_up(own, extras):
    span, cols = own.shape
    half = span // 2
    flat = [e for side in extras for e in side]

    def kernel(_, own_ref, *refs):
        at = 0
        for k, side in enumerate(extras):
            total = own_ref[k * half : (k + 1) * half]
            for ref in refs[at : at + len(side)]:
                total = total + ref[...].astype(F32)
            at += len(side)
            refs[-1][k * half : (k + 1) * half] = total.astype(BF16)

    return call(
        kernel,
        (1,),
        jnp.zeros((1,), jnp.int32),
        [own] + flat,
        [whole(own.shape)] + [whole(e.shape) for e in flat],
        jax.ShapeDtypeStruct(own.shape, BF16),
        whole(own.shape),
        [],
        "add_up",
    )


def exchange(piece):
    groups = lax.axis_size("ctx")

    def send(slot):
        route = [(i, partner(i, slot, groups)) for i in range(groups)]
        return lax.ppermute(piece(slot), "ctx", route)

    return [piece(0)] + [send(s) for s in range(1, groups)]


def in_order(blocks, me):
    groups = len(blocks)
    result = jnp.zeros((groups,) + blocks[0].shape, blocks[0].dtype)
    for s, b in enumerate(blocks):
        result = lax.dynamic_update_index_in_dim(result, b, source(me, s, groups), 0)
    return jnp.concatenate(list(result), 1)


def taps_spectra_plain(pieces, forward, back, me):
    groups = len(pieces)
    span, share = pieces[0].shape
    taps = in_order(pieces, me)
    before = jnp.concatenate(
        [jnp.zeros((span, share), BF16), taps[:, : (groups - 1) * share]], 1
    )
    before = jnp.where(lax.broadcasted_iota(jnp.int32, (span, 1), 0) == 0, 0, before)
    spectra = dot(forward, jnp.concatenate([taps, before], 0)).astype(BF16)
    return spectra, forward[:, :span], back


def long_filter_plain(pieces, taps, spectra_taps, forward_in, back, skip, me):
    groups = len(pieces)
    span, share = back.shape[0], pieces[0].shape[1]
    pieces = in_order(pieces, me)
    tails = [pieces[span + t * EDGE : span + (t + 1) * EDGE] for t in (0, 1)]
    heads = []
    for t in (0, 1):
        before = jnp.concatenate([jnp.zeros((EDGE, share), BF16), tails[t][:, :-share]], 1)
        wide = [jnp.tile(taps[lag, t + 1], (1, groups)) for lag in range(KERNEL)]
        heads.append(first_rows(wide, before, tails[t]))
    signal = jnp.concatenate([gated(*heads), pieces[8:span]], 0)
    spectra = dot(forward_in, signal).astype(BF16)
    real_g, imag_g = spectra_taps[:span].astype(F32), spectra_taps[span:].astype(F32)
    real_u, imag_u = spectra[:span].astype(F32), spectra[span:].astype(F32)
    first = lax.broadcasted_iota(jnp.int32, (span, 1), 0) == 0
    mixed = []
    for i in range(groups):
        real = imag = 0.0
        for j in range(i + 1):
            g = slice((i - j) * share, (i - j + 1) * share)
            u = slice(j * share, (j + 1) * share)
            rr = real_g[:, g] * real_u[:, u]
            ii = imag_g[:, g] * imag_u[:, u]
            cross = real_g[:, g] * imag_u[:, u] + imag_g[:, g] * real_u[:, u]
            real = real + jnp.where(first, rr, rr - ii)
            imag = imag + jnp.where(first, ii, cross)
        mixed.append(jnp.concatenate([real, imag], 0).astype(BF16))
    result = dot(back, jnp.concatenate(mixed, 1)) + skip * signal.astype(F32)
    result = jnp.stack(jnp.split(result.astype(BF16), groups, axis=1))
    found = []
    for s in range(groups):
        block = lax.dynamic_index_in_dim(result, partner(me, s, groups), 0, keepdims=False)
        found.append(block)
    return found


def gate_blocks_plain(gate, before, here, taps, pieces, me):
    head = first_rows([taps[lag, 0] for lag in range(KERNEL)], before, here)
    return gated(jnp.concatenate([head, gate[8:]], 0), in_order(pieces, me))


def body(inputs, w_in, conv_taps, skip_gain, filter_taps, w_out):
    span, width = inputs.shape
    half = span // 2
    groups = lax.axis_size("ctx")
    me = lax.axis_index("ctx")
    chips = lax.axis_size("chan") // 2
    reach = chips // 2
    place = lax.axis_index("chan")
    chip, core = place // 2, place % 2
    share = width // groups
    aligned = share % 128 == 0
    out_width = w_out.shape[1] // (2 * chips)
    forward_np, back_np = half_tables(span)
    forward, back = jnp.asarray(forward_np), jnp.asarray(back_np)
    forward_in = jnp.asarray(np.ascontiguousarray(forward_np[:, :span]))
    w_streams = jnp.transpose(w_in, (1, 0, 2))
    short_taps = conv_taps.astype(F32)[:, :, None]

    split_taps = [filter_taps[:, q * share : (q + 1) * share] for q in range(groups)]
    split_taps = jnp.stack(split_taps)

    def pick(stack):
        return lambda s: lax.dynamic_index_in_dim(
            stack, partner(me, s, groups), 0, keepdims=False
        )

    spectra_taps = (taps_spectra if aligned else taps_spectra_plain)(
        exchange(pick(split_taps)), forward, back, me
    )[0]
    tables = (spectra_taps,)

    def columns(w, parity):
        starts = [(2 * z + parity) * out_width for z in range(chips)]
        return jnp.concatenate([lax.dynamic_slice_in_dim(w, c, out_width, 1) for c in starts], 1)

    w_given = columns(w_out, 1 - core)
    w_far = lax.dynamic_slice_in_dim(w_streams, (chip + reach) % chips * 2 * width, 2 * width, 1)

    skip = lax.dynamic_slice_in_dim(skip_gain, me * share, share, 0)
    skip = jnp.tile(skip, groups)[None]
    share_taps = lax.dynamic_slice_in_dim(short_taps, me * share, share, 3)

    def both(blocks):
        return blocks, [sibling(b) for b in blocks]

    found = [(0, [inputs], [sibling(inputs)])]
    upper = inputs[:half]
    up = [upper, after(inputs, upper)[half:]]
    down = list(up)
    for d in range(1, reach):
        up = [shift(u, "chan", 2) for u in up]
        down = [shift(u, "chan", -2) for u in down]
        found += [(d, *both(up)), (-d, *both(down))]
    far_top = shift(up[0], "chan", 2)
    far_low = shift(down[1], "chan", -2)
    found.append((reach, *both([far_top])))
    found[0] = (0, [after(inputs, w_given, w_far, skip, share_taps, *tables)], found[0][2])
    top, low = project_most(
        [(mine, theirs) for _, mine, theirs in found],
        [(chip - d) % chips for d, _, _ in found],
        core,
        w_streams,
    )
    far_low = after(far_low, low)
    gate, gate_ends, pieces = project_rest(
        (far_low, sibling(far_low)), core, me, w_far, top, low, short_taps, groups
    )

    pieces_in = exchange(lambda s: pieces[s])
    before = shift(after(gate_ends, pieces_in[-1]), "ctx", 1)
    before = jnp.where(me > 0, before, jnp.zeros_like(before))

    w_own = columns(after(w_out, gate), core)

    w_other = sibling(after(w_given, gate))

    filtered = (long_filter if aligned else long_filter_plain)(
        pieces_in, share_taps, *tables, forward_in, back, after(skip, w_own), me
    )
    filtered = lax.optimization_barrier((list(filtered), w_other))[0]
    gated_out = (gate_blocks if aligned else gate_blocks_plain)(
        gate, before, gate_ends, short_taps, exchange(lambda s: filtered[s]), me
    )

    other = sibling(gated_out)

    def shares(offsets, plan):
        ids = [(chip + d) % chips for d in offsets]
        return output_shares(gated_out, other, w_own, w_other, ids, plan)

    up_top, down_low = shares([reach], [[(0, half, BF16), (half, span, BF16)]])
    offsets, plan = [], []
    for d in range(reach - 1, 0, -1):
        last = d == reach - 1
        offsets += [d, -d]
        plan.append([(0, half, F32), (half, span, BF16 if last else F32)])
        plan.append([(0, half, BF16 if last else F32), (half, span, F32)])
    kept = list(shares(offsets + [0], plan + [[(0, span, F32)]]))
    up_top, down_low = shift(up_top, "chan", 2), shift(down_low, "chan", -2)
    up_low = down_top = None

    def step(carried, new, distance):
        if carried is not None:
            new = (carried.astype(F32) + new).astype(BF16)
        return shift(new, "chan", distance)

    for k in range(reach - 1):
        ahead_top, ahead_low, behind_top, behind_low = kept[4 * k : 4 * k + 4]
        up_low, down_top = step(up_low, ahead_low, 2), step(down_top, behind_top, -2)
        up_top, down_low = step(up_top, ahead_top, 2), step(down_low, behind_low, -2)
    extras = [[up_top], [down_low]]
    if reach > 1:
        extras = [[up_top, down_top], [up_low, down_low]]
    return add_up(kept[-1], extras)


def solution(mesh):
    return jax.shard_map(
        body,
        mesh=mesh,
        in_specs=(
            P("ctx", "chan"),
            P(None, None, "chan"),
            P(None, None, "chan"),
            P("chan"),
            P("ctx", "chan"),
            P("chan", None),
        ),
        out_specs=P("ctx", "chan"),
        check_vma=False,
    )
```

```python
import math

import jax
import jax.numpy as jnp
import ml_dtypes
import numpy as np
from jax import lax
from jax.experimental import pallas as pl
from jax.experimental.pallas import tpu as pltpu
from jax.sharding import PartitionSpec as P

KERNEL = 3
EDGE = 16
BF16 = jnp.bfloat16
F32 = jnp.float32
MIB = 1 << 20


def half_tables(span):
    n = 2 * span
    f = np.arange(span)[:, None]
    m = np.arange(n)[None, :]
    ang = 2.0 * math.pi * ((f * m) % n) / n
    real = np.cos(ang)
    imag = -np.sin(ang)
    imag[0] = np.where(np.arange(n) % 2 == 0, 1.0, -1.0)
    forward = np.concatenate([real, imag], 0).astype(ml_dtypes.bfloat16)
    weight = np.full((n, 1), 2.0 / n)
    weight[0] = 1.0 / n
    weight[span] = 1.0 / n
    back = (np.concatenate([real, imag], 0) * weight)[:, :span].T
    return forward, np.ascontiguousarray(back).astype(ml_dtypes.bfloat16)


def shift(x, axis, distance):
    size = lax.axis_size(axis)
    return lax.ppermute(x, axis, [(i, (i + distance) % size) for i in range(size)])


def sibling(x):
    return lax.ppermute(x, "chan", [(i, i ^ 1) for i in range(lax.axis_size("chan"))])


def dot(a, b):
    return jnp.dot(a, b, preferred_element_type=F32)


def after(x, *others):
    return lax.optimization_barrier((x,) + others)[0]


def anywhere():
    return pl.BlockSpec(memory_space=pl.ANY)


def whole(shape):
    return pl.BlockSpec(shape, lambda *_: (0,) * len(shape))


def call(kernel, grid, prefetch, operands, in_specs, outs, out_specs, scratch, name, micros=1, vmem=16):
    return pl.pallas_call(
        kernel,
        grid_spec=pltpu.PrefetchScalarGridSpec(
            num_scalar_prefetch=1,
            grid=grid,
            in_specs=in_specs,
            out_specs=out_specs,
            scratch_shapes=scratch,
        ),
        out_shape=outs,
        compiler_params=pltpu.CompilerParams(vmem_limit_bytes=vmem * MIB),
        cost_estimate=pl.CostEstimate(
            flops=micros * 10**9, bytes_accessed=micros << 20, transcendentals=0
        ),
        name=name,
    )(prefetch, *operands)


def short_filter(taps, before, block):
    longer = jnp.concatenate([before, block], 0)
    rows = block.shape[0]
    result = jnp.zeros(block.shape, F32)
    for lag in range(KERNEL):
        result = result + taps[lag] * longer[8 - lag : 8 - lag + rows]
    return result.astype(BF16)


def first_rows(taps, before, here):
    return short_filter(taps, before[8:].astype(F32), here[:8].astype(F32))


def gated(gate_in, values):
    return (gate_in.astype(F32) * values.astype(F32)).astype(BF16)


def start_copies(copies):
    for copy in copies:
        copy.start()


def wait_copies(copies):
    for copy in copies:
        copy.wait()


def project_most(pairs, chip_ids, core, w_in):
    count = len(pairs)
    parts = [p for pair in pairs for block in pair for p in block]
    rows = sum(p.shape[0] for p in pairs[0][0])
    half = rows // 2
    width = parts[0].shape[1]
    streams, _, out_width = w_in.shape
    depth = 2 * width
    most = (count - 1) * depth

    def kernel(ids, w_ref, *refs):
        part_refs, refs = refs[: len(parts)], refs[len(parts) :]
        top_ref, low_ref, x, far, w, x_ready, w_ready = refs
        s = pl.program_id(0)

        def w_copies(t):
            for j in range(count):
                first = pl.multiple_of(ids[j] * depth, depth)
                yield pltpu.make_async_copy(
                    w_ref.at[t, pl.ds(first, depth)],
                    w.at[t, j * depth : (j + 1) * depth],
                    w_ready.at[t, j],
                )

        def x_copies():
            at = 0
            for j in range(count):
                for block, side in ((pairs[j][0], ids[count]), (pairs[j][1], 1 - ids[count])):
                    row = 0
                    base = j * depth if j < count - 1 else 0
                    place = pl.ds(pl.multiple_of(base + side * width, width), width)
                    for part in block:
                        target = (x if j < count - 1 else far).at[row : row + part.shape[0], place]
                        yield pltpu.make_async_copy(part_refs[at], target, x_ready.at[at])
                        row += part.shape[0]
                        at += 1

        @pl.when(s == 0)
        def _():
            start_copies(w_copies(0))
            start_copies(x_copies())
            for t in range(1, streams):
                start_copies(w_copies(t))
            wait_copies(x_copies())

        wait_copies(w_copies(s))
        total = dot(x[...], w[s, :most])
        top_ref[0] = (total[:half] + dot(far[...], w[s, most:])).astype(BF16)
        low_ref[0] = total[half:]

    def by_stream():
        return pl.BlockSpec((1, half, out_width), lambda s, ids: (s, 0, 0))

    shape = (streams, half, out_width)
    return call(
        kernel,
        (streams,),
        jnp.stack(list(chip_ids) + [core]).astype(jnp.int32),
        [w_in] + parts,
        [anywhere()] * (1 + len(parts)),
        [jax.ShapeDtypeStruct(shape, BF16), jax.ShapeDtypeStruct(shape, F32)],
        [by_stream(), by_stream()],
        [
            pltpu.VMEM((rows, most), BF16),
            pltpu.VMEM((half, depth), BF16),
            pltpu.VMEM((streams, most + depth, out_width), BF16),
            pltpu.SemaphoreType.DMA((len(parts),)),
            pltpu.SemaphoreType.DMA((streams, count)),
        ],
        "project_most",
        20,
        24,
    )


def project_rest(pair, core, me, w_far, top, low, conv_taps, groups):
    streams, half, out_width = top.shape
    rows = 2 * half
    width = pair[0].shape[1]
    depth = 2 * width
    share = out_width // groups
    split = share % 128 == 0
    order = list(range(1, streams)) + [0]

    def kernel(at, own_ref, other_ref, w_ref, top_ref, low_ref, taps_ref, gate_ref, ends_ref, *refs):
        in_refs, refs = refs[: len(ins)], refs[len(ins) :]
        x, w, tops, lows, kept, x_ready, ready = refs

        def x_copies():
            for k, (ref, side) in enumerate(((own_ref, at[0]), (other_ref, 1 - at[0]))):
                place = pl.ds(pl.multiple_of(side * width, width), width)
                yield pltpu.make_async_copy(ref, x.at[:, place], x_ready.at[k])

        def copies(t):
            for k, (ref, target) in enumerate(((w_ref, w), (low_ref, lows), (top_ref, tops))):
                yield pltpu.make_async_copy(ref.at[t], target.at[t], ready.at[t, k])

        start_copies(x_copies())
        for t in order:
            start_copies(copies(t))
        wait_copies(x_copies())
        for t in order:
            wait_copies(copies(t))
            bottom = (dot(x[...], w[t]) + lows[t]).astype(BF16)
            upper = tops[t]
            taps = [taps_ref[lag, t] for lag in range(KERNEL)]
            first = upper.astype(F32)
            kept[t, :half] = short_filter(taps, jnp.zeros((8, out_width), F32), first)
            kept[t, half:rows] = short_filter(taps, first[half - 8 :], bottom.astype(F32))
            ends = jnp.concatenate([first[:8], bottom.astype(F32)[half - 8 :]], 0)
            kept[t, rows:] = ends.astype(BF16)
        gate_ref[...] = kept[0, :rows]
        ends_ref[...] = kept[0, rows:]
        kept[0, :rows] = gated(kept[1, :rows], kept[2, :rows])
        for slot in range(len(ins)):
            q = pl.multiple_of(partner(at[1], slot, groups) * share, share)
            columns = pl.ds(q, share) if split else slice(None)
            in_refs[slot][:rows] = kept[0, :rows, columns]
            for t in range(1, streams):
                place = rows + (t - 1) * EDGE
                in_refs[slot][place : place + EDGE] = kept[t, rows:, columns]

    longer = rows + (streams - 1) * EDGE
    ins = [pltpu.HBM((longer, share if split else out_width), BF16)] * (groups if split else 1)
    outs = [pltpu.HBM((rows, out_width), BF16), pltpu.HBM((EDGE, out_width), BF16)] + ins
    found = call(
        kernel,
        (1,),
        jnp.stack([core, me]).astype(jnp.int32),
        list(pair) + [w_far, top, low, conv_taps],
        [anywhere()] * 5 + [whole(conv_taps.shape)],
        outs,
        [whole(o.shape) for o in outs],
        [
            pltpu.VMEM((half, depth), BF16),
            pltpu.VMEM(w_far.shape, BF16),
            pltpu.VMEM(top.shape, BF16),
            pltpu.VMEM(low.shape, F32),
            pltpu.VMEM((streams, rows + EDGE, out_width), BF16),
            pltpu.SemaphoreType.DMA((2,)),
            pltpu.SemaphoreType.DMA((streams, 3)),
        ],
        "project_rest",
        4,
        24,
    )
    gate, ends, ins = found[0], found[1], list(found[2:])
    return gate, ends, (ins if split else by_slot(ins[0], groups, me))


def by_slot(block, groups, me):
    stack = jnp.stack(jnp.split(block, groups, axis=1))
    return [
        lax.dynamic_index_in_dim(stack, partner(me, slot, groups), 0, keepdims=False)
        for slot in range(groups)
    ]


def partner(me, slot, groups):
    if groups & (groups - 1) == 0:
        return me ^ slot
    return (me + slot) % groups


def source(me, slot, groups):
    if groups & (groups - 1) == 0:
        return me ^ slot
    return (me - slot + groups) % groups


def taps_spectra(pieces, forward, back, me):
    groups = len(pieces)
    span, share = pieces[0].shape

    def kernel(at, *refs):
        piece_refs, refs = refs[:groups], refs[groups:]
        forward_ref, out_ref, padded = refs
        row_ids = lax.broadcasted_iota(jnp.int32, (span, share), 0)
        for s in range(groups):
            k = source(at[0], s, groups)
            block = piece_refs[s][...]
            padded[0:span, pl.ds(pl.multiple_of(k * share, share), share)] = block

            @pl.when(k < groups - 1)
            def _():
                place = pl.multiple_of((k + 1) * share, share)
                kept = jnp.where(row_ids == 0, 0.0, block.astype(F32)).astype(BF16)
                padded[span : 2 * span, pl.ds(place, share)] = kept

        padded[span : 2 * span, 0:share] = jnp.zeros((span, share), BF16)
        out_ref[...] = dot(forward_ref[...], padded[...]).astype(BF16)

    shape = (2 * span, groups * share)
    outs = [pltpu.HBM(shape, BF16)]
    operands = list(pieces) + [forward]
    (spectra,) = call(
        kernel,
        (1,),
        me[None],
        operands,
        [whole(o.shape) for o in operands],
        outs,
        [whole(o.shape) for o in outs],
        [pltpu.VMEM(shape, BF16)],
        "taps_spectra",
        20,
    )
    return spectra, None, back


def long_filter(pieces, taps, spectra_taps, forward_in, back, skip, me):
    groups = len(pieces)
    share = pieces[0].shape[1]
    span = back.shape[0]
    cols = groups * share
    step = 16

    def kernel(at, *refs):
        ins, refs = refs[:groups], refs[groups:]
        short_ref, taps_ref, forward_ref, back_ref, skip_ref = refs[:5]
        outs, (signal, spectra, mixture, result, tails) = refs[5 : 5 + groups], refs[5 + groups :]
        for s in range(groups):
            j = source(at[0], s, groups)
            signal[:, pl.ds(pl.multiple_of(j * share, share), share)] = ins[s][0:span]
            tails[j] = ins[s][span:]
        for j in range(groups):
            heads = []
            for t in (0, 1):
                here = tails[j, t * EDGE : (t + 1) * EDGE]
                before = tails[j - 1, t * EDGE : (t + 1) * EDGE] if j else jnp.zeros_like(here)
                heads.append(first_rows([short_ref[lag, t + 1] for lag in range(KERNEL)], before, here))
            place = slice(j * share, (j + 1) * share)
            rest = signal[0:EDGE, place].astype(F32)[8:]
            head = jnp.concatenate([gated(*heads).astype(F32), rest], 0)
            signal[0:EDGE, place] = head.astype(BF16)
        spectra[...] = dot(forward_ref[...], signal[...]).astype(BF16)

        def mix(start, special):
            def read(ref, first, block):
                return ref[pl.ds(first, step), block * share : (block + 1) * share].astype(F32)

            imag_start = start + span
            real_g = [read(taps_ref, start, b) for b in range(groups)]
            imag_g = [read(taps_ref, imag_start, b) for b in range(groups)]
            real_u = [read(spectra, start, b) for b in range(groups)]
            imag_u = [read(spectra, imag_start, b) for b in range(groups)]
            first = lax.broadcasted_iota(jnp.int32, (step, share), 0) == 0
            for i in range(groups):
                real = imag = None
                for j in range(i + 1):
                    rr = real_g[i - j] * real_u[j]
                    ii = imag_g[i - j] * imag_u[j]
                    cross = real_g[i - j] * imag_u[j] + imag_g[i - j] * real_u[j]
                    new_real, new_imag = rr - ii, cross
                    if special:
                        new_real = jnp.where(first, rr, new_real)
                        new_imag = jnp.where(first, ii, new_imag)
                    real = new_real if real is None else real + new_real
                    imag = new_imag if imag is None else imag + new_imag
                place = slice(i * share, (i + 1) * share)
                mixture[pl.ds(start, step), place] = real.astype(BF16)
                mixture[pl.ds(imag_start, step), place] = imag.astype(BF16)

        mix(0, True)

        @pl.loop(1, span // step)
        def _(c):
            mix(pl.multiple_of(c * step, step), False)

        result[...] = (
            dot(back_ref[...], mixture[...]) + skip_ref[...] * signal[...].astype(F32)
        ).astype(BF16)
        for s in range(groups):
            j = pl.multiple_of(partner(at[0], s, groups) * share, share)
            outs[s][...] = result[:, pl.ds(j, share)]

    operands = list(pieces) + [taps, spectra_taps, forward_in, back, skip]
    in_specs = [whole(o.shape) for o in operands]
    outs = [jax.ShapeDtypeStruct((span, share), BF16)] * groups
    return call(
        kernel,
        (1,),
        me[None],
        operands,
        in_specs,
        outs,
        [whole(o.shape) for o in outs],
        [
            pltpu.VMEM((span, cols), BF16),
            pltpu.VMEM((2 * span, cols), BF16),
            pltpu.VMEM((2 * span, cols), BF16),
            pltpu.VMEM((span, cols), BF16),
            pltpu.VMEM((groups, 2 * EDGE, share), BF16),
        ],
        "long_filter",
        6,
    )


def gate_blocks(gate, before, here, taps, pieces, me):
    groups = len(pieces)
    rows, share = pieces[0].shape

    def kernel(at, gate_ref, before_ref, here_ref, taps_ref, *refs):
        out = refs[groups]
        head = first_rows([taps_ref[lag, 0] for lag in range(KERNEL)], before_ref[...], here_ref[...])
        rest = gate_ref[0:EDGE].astype(F32)[8:]
        edge_ref = refs[groups + 1]
        edge_ref[...] = jnp.concatenate([head.astype(F32), rest], 0).astype(BF16)
        for s in range(groups):
            place = pl.ds(pl.multiple_of(source(at[0], s, groups) * share, share), share)
            out[:, place] = gated(gate_ref[:, place], refs[s][...])
            out[0:EDGE, place] = gated(edge_ref[:, place], refs[s][0:EDGE])

    operands = [gate, before, here, taps] + list(pieces)
    return call(
        kernel,
        (1,),
        me[None],
        operands,
        [whole(o.shape) for o in operands],
        jax.ShapeDtypeStruct(gate.shape, BF16),
        whole(gate.shape),
        [pltpu.VMEM(here.shape, BF16)],
        "gate_blocks",
        3,
    )


def output_shares(gated, other, w_own, w_other, chip_ids, plan):
    count = len(chip_ids)
    rows, width = gated.shape
    cols = w_other.shape[1] * 2 // lax.axis_size("chan")

    def kernel(_, a_ref, b_ref, w_ref, v_ref, *outs):
        k = pl.program_id(0)
        total = dot(a_ref[...], w_ref[...]) + dot(b_ref[...], v_ref[...])
        at = 0
        for j in range(count):
            here = outs[at : at + len(plan[j])]
            at += len(plan[j])

            @pl.when(k == j)
            def _():
                for out, (first, last, kind) in zip(here, plan[j]):
                    out[...] = total[first:last].astype(kind)

    outs = [
        jax.ShapeDtypeStruct((last - first, cols), kind)
        for parts in plan
        for first, last, kind in parts
    ]
    return call(
        kernel,
        (count,),
        jnp.stack(list(chip_ids)).astype(jnp.int32),
        [gated, other, w_own, w_other],
        [
            whole(gated.shape),
            whole(other.shape),
            pl.BlockSpec((width, cols), lambda k, ids: (0, ids[k])),
            pl.BlockSpec((width, cols), lambda k, ids: (0, ids[k])),
        ],
        outs,
        [whole(o.shape) for o in outs],
        [],
        "output_shares",
        1,
    )


def add_up(own, extras):
    span, cols = own.shape
    half = span // 2
    flat = [e for side in extras for e in side]

    def kernel(_, own_ref, *refs):
        at = 0
        for k, side in enumerate(extras):
            total = own_ref[k * half : (k + 1) * half]
            for ref in refs[at : at + len(side)]:
                total = total + ref[...].astype(F32)
            at += len(side)
            refs[-1][k * half : (k + 1) * half] = total.astype(BF16)

    return call(
        kernel,
        (1,),
        jnp.zeros((1,), jnp.int32),
        [own] + flat,
        [whole(own.shape)] + [whole(e.shape) for e in flat],
        jax.ShapeDtypeStruct(own.shape, BF16),
        whole(own.shape),
        [],
        "add_up",
    )


def exchange(piece, chained=False):
    groups = lax.axis_size("ctx")
    found = [piece(0)]
    for slot in range(1, groups):
        route = [(i, partner(i, slot, groups)) for i in range(groups)]
        block = piece(slot)
        if chained and slot > 1:
            block = after(block, found[-1])
        found.append(lax.ppermute(block, "ctx", route))
    return found


def in_order(blocks, me):
    groups = len(blocks)
    result = jnp.zeros((groups,) + blocks[0].shape, blocks[0].dtype)
    for s, b in enumerate(blocks):
        result = lax.dynamic_update_index_in_dim(result, b, source(me, s, groups), 0)
    return jnp.concatenate(list(result), 1)


def taps_spectra_plain(pieces, forward, back, me):
    groups = len(pieces)
    span, share = pieces[0].shape
    taps = in_order(pieces, me)
    before = jnp.concatenate(
        [jnp.zeros((span, share), BF16), taps[:, : (groups - 1) * share]], 1
    )
    before = jnp.where(lax.broadcasted_iota(jnp.int32, (span, 1), 0) == 0, 0, before)
    spectra = dot(forward, jnp.concatenate([taps, before], 0)).astype(BF16)
    return spectra, forward[:, :span], back


def long_filter_plain(pieces, taps, spectra_taps, forward_in, back, skip, me):
    groups = len(pieces)
    span, share = back.shape[0], pieces[0].shape[1]
    pieces = in_order(pieces, me)
    tails = [pieces[span + t * EDGE : span + (t + 1) * EDGE] for t in (0, 1)]
    heads = []
    for t in (0, 1):
        before = jnp.concatenate([jnp.zeros((EDGE, share), BF16), tails[t][:, :-share]], 1)
        wide = [jnp.tile(taps[lag, t + 1], (1, groups)) for lag in range(KERNEL)]
        heads.append(first_rows(wide, before, tails[t]))
    signal = jnp.concatenate([gated(*heads), pieces[8:span]], 0)
    spectra = dot(forward_in, signal).astype(BF16)
    real_g, imag_g = spectra_taps[:span].astype(F32), spectra_taps[span:].astype(F32)
    real_u, imag_u = spectra[:span].astype(F32), spectra[span:].astype(F32)
    first = lax.broadcasted_iota(jnp.int32, (span, 1), 0) == 0
    mixed = []
    for i in range(groups):
        real = imag = 0.0
        for j in range(i + 1):
            g = slice((i - j) * share, (i - j + 1) * share)
            u = slice(j * share, (j + 1) * share)
            rr = real_g[:, g] * real_u[:, u]
            ii = imag_g[:, g] * imag_u[:, u]
            cross = real_g[:, g] * imag_u[:, u] + imag_g[:, g] * real_u[:, u]
            real = real + jnp.where(first, rr, rr - ii)
            imag = imag + jnp.where(first, ii, cross)
        mixed.append(jnp.concatenate([real, imag], 0).astype(BF16))
    result = dot(back, jnp.concatenate(mixed, 1)) + skip * signal.astype(F32)
    result = jnp.stack(jnp.split(result.astype(BF16), groups, axis=1))
    found = []
    for s in range(groups):
        block = lax.dynamic_index_in_dim(result, partner(me, s, groups), 0, keepdims=False)
        found.append(block)
    return found


def gate_blocks_plain(gate, before, here, taps, pieces, me):
    head = first_rows([taps[lag, 0] for lag in range(KERNEL)], before, here)
    return gated(jnp.concatenate([head, gate[8:]], 0), in_order(pieces, me))


def body(inputs, w_in, conv_taps, skip_gain, filter_taps, w_out):
    span, width = inputs.shape
    half = span // 2
    groups = lax.axis_size("ctx")
    me = lax.axis_index("ctx")
    chips = lax.axis_size("chan") // 2
    reach = chips // 2
    place = lax.axis_index("chan")
    chip, core = place // 2, place % 2
    share = width // groups
    aligned = share % 128 == 0
    out_width = w_out.shape[1] // (2 * chips)
    forward_np, back_np = half_tables(span)
    forward, back = jnp.asarray(forward_np), jnp.asarray(back_np)
    forward_in = jnp.asarray(np.ascontiguousarray(forward_np[:, :span]))
    w_streams = jnp.transpose(w_in, (1, 0, 2))
    short_taps = conv_taps.astype(F32)[:, :, None]

    split_taps = [filter_taps[:, q * share : (q + 1) * share] for q in range(groups)]
    split_taps = jnp.stack(split_taps)

    def pick(stack):
        return lambda s: lax.dynamic_index_in_dim(
            stack, partner(me, s, groups), 0, keepdims=False
        )

    spectra_taps = (taps_spectra if aligned else taps_spectra_plain)(
        exchange(pick(split_taps), True), forward, back, me
    )[0]
    tables = (spectra_taps,)

    def columns(w, parity):
        starts = [(2 * z + parity) * out_width for z in range(chips)]
        return jnp.concatenate([lax.dynamic_slice_in_dim(w, c, out_width, 1) for c in starts], 1)

    w_given = columns(w_out, 1 - core)
    w_far = lax.dynamic_slice_in_dim(w_streams, (chip + reach) % chips * 2 * width, 2 * width, 1)

    skip = lax.dynamic_slice_in_dim(skip_gain, me * share, share, 0)
    skip = jnp.tile(skip, groups)[None]
    share_taps = lax.dynamic_slice_in_dim(short_taps, me * share, share, 3)

    def both(blocks):
        return blocks, [sibling(b) for b in blocks]

    found = [(0, [inputs], [sibling(inputs)])]
    upper = inputs[:half]
    up = [upper, after(inputs, upper)[half:]]
    down = list(up)
    for d in range(1, reach):
        up = [shift(u, "chan", 2) for u in up]
        down = [shift(u, "chan", -2) for u in down]
        found += [(d, *both(up)), (-d, *both(down))]
    far_top = shift(up[0], "chan", 2)
    far_low = shift(down[1], "chan", -2)
    found.append((reach, *both([far_top])))
    found[0] = (0, [after(inputs, w_given, w_far, skip, share_taps, *tables)], found[0][2])
    top, low = project_most(
        [(mine, theirs) for _, mine, theirs in found],
        [(chip - d) % chips for d, _, _ in found],
        core,
        w_streams,
    )
    far_low = after(far_low, low)
    gate, gate_ends, pieces = project_rest(
        (far_low, sibling(far_low)), core, me, w_far, top, low, short_taps, groups
    )

    pieces_in = exchange(lambda s: pieces[s])
    before = shift(after(gate_ends, pieces_in[1]), "ctx", 1)
    before = jnp.where(me > 0, before, jnp.zeros_like(before))

    w_own = columns(after(w_out, gate), core)

    w_other = sibling(after(w_given, gate))

    filtered = (long_filter if aligned else long_filter_plain)(
        pieces_in, share_taps, *tables, forward_in, back, after(skip, w_own), me
    )
    filtered = lax.optimization_barrier((list(filtered), w_other))[0]
    gated_out = (gate_blocks if aligned else gate_blocks_plain)(
        gate, before, gate_ends, short_taps, exchange(lambda s: filtered[s]), me
    )

    other = sibling(gated_out)

    def shares(offsets, plan):
        ids = [(chip + d) % chips for d in offsets]
        return output_shares(gated_out, other, w_own, w_other, ids, plan)

    up_top, down_low = shares([reach], [[(0, half, BF16), (half, span, BF16)]])
    offsets, plan = [], []
    for d in range(reach - 1, 0, -1):
        last = d == reach - 1
        offsets += [d, -d]
        plan.append([(0, half, F32), (half, span, BF16 if last else F32)])
        plan.append([(0, half, BF16 if last else F32), (half, span, F32)])
    kept = list(shares(offsets + [0], plan + [[(0, span, F32)]]))
    up_top, down_low = shift(up_top, "chan", 2), shift(down_low, "chan", -2)
    up_low = down_top = None

    def step(carried, new, distance):
        if carried is not None:
            new = (carried.astype(F32) + new).astype(BF16)
        return shift(new, "chan", distance)

    for k in range(reach - 1):
        ahead_top, ahead_low, behind_top, behind_low = kept[4 * k : 4 * k + 4]
        up_low, down_top = step(up_low, ahead_low, 2), step(down_top, behind_top, -2)
        up_top, down_low = step(up_top, ahead_top, 2), step(down_low, behind_low, -2)
    extras = [[up_top], [down_low]]
    if reach > 1:
        extras = [[up_top, down_top], [up_low, down_low]]
    return add_up(kept[-1], extras)


def solution(mesh):
    return jax.shard_map(
        body,
        mesh=mesh,
        in_specs=(
            P("ctx", "chan"),
            P(None, None, "chan"),
            P(None, None, "chan"),
            P("chan"),
            P("ctx", "chan"),
            P("chan", None),
        ),
        out_specs=P("ctx", "chan"),
        check_vma=False,
    )
```

```python
import math

import jax
import jax.numpy as jnp
import ml_dtypes
import numpy as np
from jax import lax
from jax.experimental import pallas as pl
from jax.experimental.pallas import tpu as pltpu
from jax.sharding import PartitionSpec as P

KERNEL = 3
EDGE = 16
BF16 = jnp.bfloat16
F32 = jnp.float32
MIB = 1 << 20


def half_tables(span):
    n = 2 * span
    f = np.arange(span)[:, None]
    m = np.arange(n)[None, :]
    ang = 2.0 * math.pi * ((f * m) % n) / n
    real = np.cos(ang)
    imag = -np.sin(ang)
    imag[0] = np.where(np.arange(n) % 2 == 0, 1.0, -1.0)
    forward = np.concatenate([real, imag], 0).astype(ml_dtypes.bfloat16)
    weight = np.full((n, 1), 2.0 / n)
    weight[0] = 1.0 / n
    weight[span] = 1.0 / n
    back = (np.concatenate([real, imag], 0) * weight)[:, :span].T
    return forward, np.ascontiguousarray(back).astype(ml_dtypes.bfloat16)


def shift(x, axis, distance):
    size = lax.axis_size(axis)
    return lax.ppermute(x, axis, [(i, (i + distance) % size) for i in range(size)])


def sibling(x):
    return lax.ppermute(x, "chan", [(i, i ^ 1) for i in range(lax.axis_size("chan"))])


def dot(a, b):
    return jnp.dot(a, b, preferred_element_type=F32)


def after(x, *others):
    return lax.optimization_barrier((x,) + others)[0]


def anywhere():
    return pl.BlockSpec(memory_space=pl.ANY)


def whole(shape):
    return pl.BlockSpec(shape, lambda *_: (0,) * len(shape))


def call(kernel, grid, prefetch, operands, in_specs, outs, out_specs, scratch, name, micros=1, vmem=16):
    return pl.pallas_call(
        kernel,
        grid_spec=pltpu.PrefetchScalarGridSpec(
            num_scalar_prefetch=1,
            grid=grid,
            in_specs=in_specs,
            out_specs=out_specs,
            scratch_shapes=scratch,
        ),
        out_shape=outs,
        compiler_params=pltpu.CompilerParams(vmem_limit_bytes=vmem * MIB),
        cost_estimate=pl.CostEstimate(
            flops=micros * 10**9, bytes_accessed=micros << 20, transcendentals=0
        ),
        name=name,
    )(prefetch, *operands)


def short_filter(taps, before, block):
    longer = jnp.concatenate([before, block], 0)
    rows = block.shape[0]
    result = jnp.zeros(block.shape, F32)
    for lag in range(KERNEL):
        result = result + taps[lag] * longer[8 - lag : 8 - lag + rows]
    return result.astype(BF16)


def first_rows(taps, before, here):
    return short_filter(taps, before[8:].astype(F32), here[:8].astype(F32))


def gated(gate_in, values):
    return (gate_in.astype(F32) * values.astype(F32)).astype(BF16)


def start_copies(copies):
    for copy in copies:
        copy.start()


def wait_copies(copies):
    for copy in copies:
        copy.wait()


def project_most(pairs, chip_ids, core, w_in):
    count = len(pairs)
    parts = [p for pair in pairs for block in pair for p in block]
    rows = sum(p.shape[0] for p in pairs[0][0])
    half = rows // 2
    width = parts[0].shape[1]
    streams, _, out_width = w_in.shape
    depth = 2 * width
    most = (count - 1) * depth

    def kernel(ids, w_ref, *refs):
        part_refs, refs = refs[: len(parts)], refs[len(parts) :]
        top_ref, low_ref, x, far, w, x_ready, w_ready = refs
        s = pl.program_id(0)

        def w_copies(t):
            for j in range(count):
                first = pl.multiple_of(ids[j] * depth, depth)
                yield pltpu.make_async_copy(
                    w_ref.at[t, pl.ds(first, depth)],
                    w.at[t, j * depth : (j + 1) * depth],
                    w_ready.at[t, j],
                )

        def x_copies():
            at = 0
            for j in range(count):
                for block, side in ((pairs[j][0], ids[count]), (pairs[j][1], 1 - ids[count])):
                    row = 0
                    base = j * depth if j < count - 1 else 0
                    place = pl.ds(pl.multiple_of(base + side * width, width), width)
                    for part in block:
                        target = (x if j < count - 1 else far).at[row : row + part.shape[0], place]
                        yield pltpu.make_async_copy(part_refs[at], target, x_ready.at[at])
                        row += part.shape[0]
                        at += 1

        @pl.when(s == 0)
        def _():
            start_copies(w_copies(0))
            start_copies(x_copies())
            for t in range(1, streams):
                start_copies(w_copies(t))
            wait_copies(x_copies())

        wait_copies(w_copies(s))
        total = dot(x[...], w[s, :most])
        top_ref[0] = (total[:half] + dot(far[...], w[s, most:])).astype(BF16)
        low_ref[0] = total[half:]

    def by_stream():
        return pl.BlockSpec((1, half, out_width), lambda s, ids: (s, 0, 0))

    shape = (streams, half, out_width)
    return call(
        kernel,
        (streams,),
        jnp.stack(list(chip_ids) + [core]).astype(jnp.int32),
        [w_in] + parts,
        [anywhere()] * (1 + len(parts)),
        [jax.ShapeDtypeStruct(shape, BF16), jax.ShapeDtypeStruct(shape, F32)],
        [by_stream(), by_stream()],
        [
            pltpu.VMEM((rows, most), BF16),
            pltpu.VMEM((half, depth), BF16),
            pltpu.VMEM((streams, most + depth, out_width), BF16),
            pltpu.SemaphoreType.DMA((len(parts),)),
            pltpu.SemaphoreType.DMA((streams, count)),
        ],
        "project_most",
        20,
        24,
    )


def project_rest(pair, core, me, w_far, top, low, conv_taps, groups):
    streams, half, out_width = top.shape
    rows = 2 * half
    width = pair[0].shape[1]
    depth = 2 * width
    share = out_width // groups
    split = share % 128 == 0
    order = list(range(1, streams)) + [0]

    def kernel(at, own_ref, other_ref, w_ref, top_ref, low_ref, taps_ref, gate_ref, ends_ref, *refs):
        in_refs, refs = refs[: len(ins)], refs[len(ins) :]
        x, w, tops, lows, kept, x_ready, ready = refs

        def x_copies():
            for k, (ref, side) in enumerate(((own_ref, at[0]), (other_ref, 1 - at[0]))):
                place = pl.ds(pl.multiple_of(side * width, width), width)
                yield pltpu.make_async_copy(ref, x.at[:, place], x_ready.at[k])

        def copies(t):
            for k, (ref, target) in enumerate(((w_ref, w), (low_ref, lows), (top_ref, tops))):
                yield pltpu.make_async_copy(ref.at[t], target.at[t], ready.at[t, k])

        start_copies(x_copies())
        for t in order:
            start_copies(copies(t))
        wait_copies(x_copies())
        for t in order:
            wait_copies(copies(t))
            bottom = (dot(x[...], w[t]) + lows[t]).astype(BF16)
            upper = tops[t]
            taps = [taps_ref[lag, t] for lag in range(KERNEL)]
            first = upper.astype(F32)
            kept[t, :half] = short_filter(taps, jnp.zeros((8, out_width), F32), first)
            kept[t, half:rows] = short_filter(taps, first[half - 8 :], bottom.astype(F32))
            ends = jnp.concatenate([first[:8], bottom.astype(F32)[half - 8 :]], 0)
            kept[t, rows:] = ends.astype(BF16)
        gate_ref[...] = kept[0, :rows]
        ends_ref[...] = kept[0, rows:]
        kept[0, :rows] = gated(kept[1, :rows], kept[2, :rows])
        for slot in range(len(ins)):
            q = pl.multiple_of(partner(at[1], slot, groups) * share, share)
            columns = pl.ds(q, share) if split else slice(None)
            in_refs[slot][:rows] = kept[0, :rows, columns]
            for t in range(1, streams):
                place = rows + (t - 1) * EDGE
                in_refs[slot][place : place + EDGE] = kept[t, rows:, columns]

    longer = rows + (streams - 1) * EDGE
    ins = [pltpu.HBM((longer, share if split else out_width), BF16)] * (groups if split else 1)
    outs = [pltpu.HBM((rows, out_width), BF16), pltpu.HBM((EDGE, out_width), BF16)] + ins
    found = call(
        kernel,
        (1,),
        jnp.stack([core, me]).astype(jnp.int32),
        list(pair) + [w_far, top, low, conv_taps],
        [anywhere()] * 5 + [whole(conv_taps.shape)],
        outs,
        [whole(o.shape) for o in outs],
        [
            pltpu.VMEM((half, depth), BF16),
            pltpu.VMEM(w_far.shape, BF16),
            pltpu.VMEM(top.shape, BF16),
            pltpu.VMEM(low.shape, F32),
            pltpu.VMEM((streams, rows + EDGE, out_width), BF16),
            pltpu.SemaphoreType.DMA((2,)),
            pltpu.SemaphoreType.DMA((streams, 3)),
        ],
        "project_rest",
        4,
        24,
    )
    gate, ends, ins = found[0], found[1], list(found[2:])
    return gate, ends, (ins if split else by_slot(ins[0], groups, me))


def by_slot(block, groups, me):
    stack = jnp.stack(jnp.split(block, groups, axis=1))
    return [
        lax.dynamic_index_in_dim(stack, partner(me, slot, groups), 0, keepdims=False)
        for slot in range(groups)
    ]


def partner(me, slot, groups):
    if groups & (groups - 1) == 0:
        return me ^ slot
    return (me + slot) % groups


def source(me, slot, groups):
    if groups & (groups - 1) == 0:
        return me ^ slot
    return (me - slot + groups) % groups


def taps_spectra(pieces, forward, back, me):
    groups = len(pieces)
    span, share = pieces[0].shape

    def kernel(at, *refs):
        piece_refs, refs = refs[:groups], refs[groups:]
        forward_ref, out_ref, padded = refs
        row_ids = lax.broadcasted_iota(jnp.int32, (span, share), 0)
        for s in range(groups):
            k = source(at[0], s, groups)
            block = piece_refs[s][...]
            padded[0:span, pl.ds(pl.multiple_of(k * share, share), share)] = block

            @pl.when(k < groups - 1)
            def _():
                place = pl.multiple_of((k + 1) * share, share)
                kept = jnp.where(row_ids == 0, 0.0, block.astype(F32)).astype(BF16)
                padded[span : 2 * span, pl.ds(place, share)] = kept

        padded[span : 2 * span, 0:share] = jnp.zeros((span, share), BF16)
        out_ref[...] = dot(forward_ref[...], padded[...]).astype(BF16)

    shape = (2 * span, groups * share)
    outs = [pltpu.HBM(shape, BF16)]
    operands = list(pieces) + [forward]
    (spectra,) = call(
        kernel,
        (1,),
        me[None],
        operands,
        [whole(o.shape) for o in operands],
        outs,
        [whole(o.shape) for o in outs],
        [pltpu.VMEM(shape, BF16)],
        "taps_spectra",
        20,
    )
    return spectra, None, back


def long_filter(pieces, taps, spectra_taps, forward_in, back, skip, me):
    groups = len(pieces)
    share = pieces[0].shape[1]
    span = back.shape[0]
    cols = groups * share
    step = 16

    def kernel(at, *refs):
        ins, refs = refs[:groups], refs[groups:]
        short_ref, taps_ref, forward_ref, back_ref, skip_ref = refs[:5]
        outs, (signal, spectra, mixture, result, tails) = refs[5 : 5 + groups], refs[5 + groups :]
        for s in range(groups):
            j = source(at[0], s, groups)
            signal[:, pl.ds(pl.multiple_of(j * share, share), share)] = ins[s][0:span]
            tails[j] = ins[s][span:]
        for j in range(groups):
            heads = []
            for t in (0, 1):
                here = tails[j, t * EDGE : (t + 1) * EDGE]
                before = tails[j - 1, t * EDGE : (t + 1) * EDGE] if j else jnp.zeros_like(here)
                heads.append(first_rows([short_ref[lag, t + 1] for lag in range(KERNEL)], before, here))
            place = slice(j * share, (j + 1) * share)
            rest = signal[0:EDGE, place].astype(F32)[8:]
            head = jnp.concatenate([gated(*heads).astype(F32), rest], 0)
            signal[0:EDGE, place] = head.astype(BF16)
        spectra[...] = dot(forward_ref[...], signal[...]).astype(BF16)

        def mix(start, special):
            def read(ref, first, block):
                return ref[pl.ds(first, step), block * share : (block + 1) * share].astype(F32)

            imag_start = start + span
            real_g = [read(taps_ref, start, b) for b in range(groups)]
            imag_g = [read(taps_ref, imag_start, b) for b in range(groups)]
            real_u = [read(spectra, start, b) for b in range(groups)]
            imag_u = [read(spectra, imag_start, b) for b in range(groups)]
            first = lax.broadcasted_iota(jnp.int32, (step, share), 0) == 0
            for i in range(groups):
                real = imag = None
                for j in range(i + 1):
                    rr = real_g[i - j] * real_u[j]
                    ii = imag_g[i - j] * imag_u[j]
                    cross = real_g[i - j] * imag_u[j] + imag_g[i - j] * real_u[j]
                    new_real, new_imag = rr - ii, cross
                    if special:
                        new_real = jnp.where(first, rr, new_real)
                        new_imag = jnp.where(first, ii, new_imag)
                    real = new_real if real is None else real + new_real
                    imag = new_imag if imag is None else imag + new_imag
                place = slice(i * share, (i + 1) * share)
                mixture[pl.ds(start, step), place] = real.astype(BF16)
                mixture[pl.ds(imag_start, step), place] = imag.astype(BF16)

        mix(0, True)

        @pl.loop(1, span // step)
        def _(c):
            mix(pl.multiple_of(c * step, step), False)

        result[...] = (
            dot(back_ref[...], mixture[...]) + skip_ref[...] * signal[...].astype(F32)
        ).astype(BF16)
        for s in range(groups):
            j = pl.multiple_of(partner(at[0], s, groups) * share, share)
            outs[s][...] = result[:, pl.ds(j, share)]

    operands = list(pieces) + [taps, spectra_taps, forward_in, back, skip]
    in_specs = [whole(o.shape) for o in operands]
    outs = [jax.ShapeDtypeStruct((span, share), BF16)] * groups
    return call(
        kernel,
        (1,),
        me[None],
        operands,
        in_specs,
        outs,
        [whole(o.shape) for o in outs],
        [
            pltpu.VMEM((span, cols), BF16),
            pltpu.VMEM((2 * span, cols), BF16),
            pltpu.VMEM((2 * span, cols), BF16),
            pltpu.VMEM((span, cols), BF16),
            pltpu.VMEM((groups, 2 * EDGE, share), BF16),
        ],
        "long_filter",
        6,
    )


def gate_blocks(gate, before, here, taps, pieces, me):
    groups = len(pieces)
    rows, share = pieces[0].shape

    def kernel(at, gate_ref, before_ref, here_ref, taps_ref, *refs):
        out = refs[groups]
        head = first_rows([taps_ref[lag, 0] for lag in range(KERNEL)], before_ref[...], here_ref[...])
        rest = gate_ref[0:EDGE].astype(F32)[8:]
        edge_ref = refs[groups + 1]
        edge_ref[...] = jnp.concatenate([head.astype(F32), rest], 0).astype(BF16)
        for s in range(groups):
            place = pl.ds(pl.multiple_of(source(at[0], s, groups) * share, share), share)
            out[:, place] = gated(gate_ref[:, place], refs[s][...])
            out[0:EDGE, place] = gated(edge_ref[:, place], refs[s][0:EDGE])

    operands = [gate, before, here, taps] + list(pieces)
    return call(
        kernel,
        (1,),
        me[None],
        operands,
        [whole(o.shape) for o in operands],
        jax.ShapeDtypeStruct(gate.shape, BF16),
        whole(gate.shape),
        [pltpu.VMEM(here.shape, BF16)],
        "gate_blocks",
        3,
    )


def output_shares(gated, other, w_own, w_other, chip_ids, plan):
    count = len(chip_ids)
    rows, width = gated.shape
    cols = w_other.shape[1] * 2 // lax.axis_size("chan")

    def kernel(_, a_ref, b_ref, w_ref, v_ref, *outs):
        k = pl.program_id(0)
        total = dot(a_ref[...], w_ref[...]) + dot(b_ref[...], v_ref[...])
        at = 0
        for j in range(count):
            here = outs[at : at + len(plan[j])]
            at += len(plan[j])

            @pl.when(k == j)
            def _():
                for out, (first, last, kind) in zip(here, plan[j]):
                    out[...] = total[first:last].astype(kind)

    outs = [
        jax.ShapeDtypeStruct((last - first, cols), kind)
        for parts in plan
        for first, last, kind in parts
    ]
    return call(
        kernel,
        (count,),
        jnp.stack(list(chip_ids)).astype(jnp.int32),
        [gated, other, w_own, w_other],
        [
            whole(gated.shape),
            whole(other.shape),
            pl.BlockSpec((width, cols), lambda k, ids: (0, ids[k])),
            pl.BlockSpec((width, cols), lambda k, ids: (0, ids[k])),
        ],
        outs,
        [whole(o.shape) for o in outs],
        [],
        "output_shares",
        1,
    )


def add_up(own, extras):
    span, cols = own.shape
    half = span // 2
    flat = [e for side in extras for e in side]

    def kernel(_, own_ref, *refs):
        at = 0
        for k, side in enumerate(extras):
            total = own_ref[k * half : (k + 1) * half]
            for ref in refs[at : at + len(side)]:
                total = total + ref[...].astype(F32)
            at += len(side)
            refs[-1][k * half : (k + 1) * half] = total.astype(BF16)

    return call(
        kernel,
        (1,),
        jnp.zeros((1,), jnp.int32),
        [own] + flat,
        [whole(own.shape)] + [whole(e.shape) for e in flat],
        jax.ShapeDtypeStruct(own.shape, BF16),
        whole(own.shape),
        [],
        "add_up",
    )


def exchange(piece, chained=False):
    groups = lax.axis_size("ctx")
    found = [piece(0)]
    for slot in range(1, groups):
        route = [(i, partner(i, slot, groups)) for i in range(groups)]
        block = piece(slot)
        if chained and slot > 1:
            block = after(block, found[-1])
        found.append(lax.ppermute(block, "ctx", route))
    return found


def in_order(blocks, me):
    groups = len(blocks)
    result = jnp.zeros((groups,) + blocks[0].shape, blocks[0].dtype)
    for s, b in enumerate(blocks):
        result = lax.dynamic_update_index_in_dim(result, b, source(me, s, groups), 0)
    return jnp.concatenate(list(result), 1)


def taps_spectra_plain(pieces, forward, back, me):
    groups = len(pieces)
    span, share = pieces[0].shape
    taps = in_order(pieces, me)
    before = jnp.concatenate(
        [jnp.zeros((span, share), BF16), taps[:, : (groups - 1) * share]], 1
    )
    before = jnp.where(lax.broadcasted_iota(jnp.int32, (span, 1), 0) == 0, 0, before)
    spectra = dot(forward, jnp.concatenate([taps, before], 0)).astype(BF16)
    return spectra, forward[:, :span], back


def long_filter_plain(pieces, taps, spectra_taps, forward_in, back, skip, me):
    groups = len(pieces)
    span, share = back.shape[0], pieces[0].shape[1]
    pieces = in_order(pieces, me)
    tails = [pieces[span + t * EDGE : span + (t + 1) * EDGE] for t in (0, 1)]
    heads = []
    for t in (0, 1):
        before = jnp.concatenate([jnp.zeros((EDGE, share), BF16), tails[t][:, :-share]], 1)
        wide = [jnp.tile(taps[lag, t + 1], (1, groups)) for lag in range(KERNEL)]
        heads.append(first_rows(wide, before, tails[t]))
    signal = jnp.concatenate([gated(*heads), pieces[8:span]], 0)
    spectra = dot(forward_in, signal).astype(BF16)
    real_g, imag_g = spectra_taps[:span].astype(F32), spectra_taps[span:].astype(F32)
    real_u, imag_u = spectra[:span].astype(F32), spectra[span:].astype(F32)
    first = lax.broadcasted_iota(jnp.int32, (span, 1), 0) == 0
    mixed = []
    for i in range(groups):
        real = imag = 0.0
        for j in range(i + 1):
            g = slice((i - j) * share, (i - j + 1) * share)
            u = slice(j * share, (j + 1) * share)
            rr = real_g[:, g] * real_u[:, u]
            ii = imag_g[:, g] * imag_u[:, u]
            cross = real_g[:, g] * imag_u[:, u] + imag_g[:, g] * real_u[:, u]
            real = real + jnp.where(first, rr, rr - ii)
            imag = imag + jnp.where(first, ii, cross)
        mixed.append(jnp.concatenate([real, imag], 0).astype(BF16))
    result = dot(back, jnp.concatenate(mixed, 1)) + skip * signal.astype(F32)
    result = jnp.stack(jnp.split(result.astype(BF16), groups, axis=1))
    found = []
    for s in range(groups):
        block = lax.dynamic_index_in_dim(result, partner(me, s, groups), 0, keepdims=False)
        found.append(block)
    return found


def gate_blocks_plain(gate, before, here, taps, pieces, me):
    head = first_rows([taps[lag, 0] for lag in range(KERNEL)], before, here)
    return gated(jnp.concatenate([head, gate[8:]], 0), in_order(pieces, me))


def body(inputs, w_in, conv_taps, skip_gain, filter_taps, w_out):
    span, width = inputs.shape
    half = span // 2
    groups = lax.axis_size("ctx")
    me = lax.axis_index("ctx")
    chips = lax.axis_size("chan") // 2
    reach = chips // 2
    place = lax.axis_index("chan")
    chip, core = place // 2, place % 2
    share = width // groups
    aligned = share % 128 == 0
    out_width = w_out.shape[1] // (2 * chips)
    forward_np, back_np = half_tables(span)
    forward, back = jnp.asarray(forward_np), jnp.asarray(back_np)
    forward_in = jnp.asarray(np.ascontiguousarray(forward_np[:, :span]))
    w_streams = jnp.transpose(w_in, (1, 0, 2))
    short_taps = conv_taps.astype(F32)[:, :, None]

    split_taps = [filter_taps[:, q * share : (q + 1) * share] for q in range(groups)]
    split_taps = jnp.stack(split_taps)

    def pick(stack):
        return lambda s: lax.dynamic_index_in_dim(
            stack, partner(me, s, groups), 0, keepdims=False
        )

    spectra_taps = (taps_spectra if aligned else taps_spectra_plain)(
        exchange(pick(split_taps), True), forward, back, me
    )[0]
    tables = (spectra_taps,)

    def columns(w, parity):
        starts = [(2 * z + parity) * out_width for z in range(chips)]
        return jnp.concatenate([lax.dynamic_slice_in_dim(w, c, out_width, 1) for c in starts], 1)

    w_given = columns(w_out, 1 - core)
    w_far = lax.dynamic_slice_in_dim(w_streams, (chip + reach) % chips * 2 * width, 2 * width, 1)

    skip = lax.dynamic_slice_in_dim(skip_gain, me * share, share, 0)
    skip = jnp.tile(skip, groups)[None]
    share_taps = lax.dynamic_slice_in_dim(short_taps, me * share, share, 3)

    def both(blocks):
        return blocks, [sibling(b) for b in blocks]

    found = [(0, [inputs], [sibling(inputs)])]
    upper = inputs[:half]
    up = [upper, after(inputs, upper)[half:]]
    down = list(up)
    for d in range(1, reach):
        up = [shift(u, "chan", 2) for u in up]
        down = [shift(u, "chan", -2) for u in down]
        found += [(d, *both(up)), (-d, *both(down))]
    far_top = shift(up[0], "chan", 2)
    far_low = shift(down[1], "chan", -2)
    found.append((reach, *both([far_top])))
    found[0] = (0, [after(inputs, w_given, w_far, skip, share_taps, *tables)], found[0][2])
    top, low = project_most(
        [(mine, theirs) for _, mine, theirs in found],
        [(chip - d) % chips for d, _, _ in found],
        core,
        w_streams,
    )
    far_low = after(far_low, low)
    gate, gate_ends, pieces = project_rest(
        (far_low, sibling(far_low)), core, me, w_far, top, low, short_taps, groups
    )

    pieces_in = exchange(lambda s: pieces[s])
    before = shift(after(gate_ends, pieces_in[1]), "ctx", 1)
    before = jnp.where(me > 0, before, jnp.zeros_like(before))

    w_own = columns(after(w_out, gate), core)

    w_other = sibling(after(w_given, gate))

    filtered = (long_filter if aligned else long_filter_plain)(
        pieces_in, share_taps, *tables, forward_in, back, after(skip, w_own), me
    )
    filtered = lax.optimization_barrier((list(filtered), w_other))[0]
    gated_out = (gate_blocks if aligned else gate_blocks_plain)(
        gate, before, gate_ends, short_taps, exchange(lambda s: filtered[s]), me
    )

    other = sibling(gated_out)

    def shares(offsets, plan):
        ids = [(chip + d) % chips for d in offsets]
        return output_shares(gated_out, other, w_own, w_other, ids, plan)

    up_top, down_low = shares([reach], [[(0, half, BF16), (half, span, BF16)]])
    offsets, plan = [], []
    for d in range(reach - 1, 0, -1):
        last = d == reach - 1
        offsets += [d, -d]
        plan.append([(0, half, F32), (half, span, BF16 if last else F32)])
        plan.append([(0, half, BF16 if last else F32), (half, span, F32)])
    kept = list(shares(offsets, plan)) if offsets else []
    kept += list(shares([0], [[(0, span, F32)]]))
    up_top, down_low = shift(up_top, "chan", 2), shift(down_low, "chan", -2)
    up_low = down_top = None

    def step(carried, new, distance):
        if carried is not None:
            new = (carried.astype(F32) + new).astype(BF16)
        return shift(new, "chan", distance)

    for k in range(reach - 1):
        ahead_top, ahead_low, behind_top, behind_low = kept[4 * k : 4 * k + 4]
        up_low, down_top = step(up_low, ahead_low, 2), step(down_top, behind_top, -2)
        up_top, down_low = step(up_top, ahead_top, 2), step(down_low, behind_low, -2)
    extras = [[up_top], [down_low]]
    if reach > 1:
        extras = [[up_top, down_top], [up_low, down_low]]
    return add_up(kept[-1], extras)


def solution(mesh):
    return jax.shard_map(
        body,
        mesh=mesh,
        in_specs=(
            P("ctx", "chan"),
            P(None, None, "chan"),
            P(None, None, "chan"),
            P("chan"),
            P("ctx", "chan"),
            P("chan", None),
        ),
        out_specs=P("ctx", "chan"),
        check_vma=False,
    )
```
